32 devices in a mesh: segment: 4 (over y, core), dp: 8 (over z, x).
Axes of the slice: x: 2, y: 2, z: 4, core: 2. Of those that a mesh axis runs over, the one named last changes fastest.
Arguments:
- inputs: bfloat16 [2, 512, 4096], P(None, 'dp'), may hold values from -6 to 6
- cotangent: bfloat16 [2, 512, 4096], P(None, 'dp'), may hold values from -2 to 2
- w_in: bfloat16 [4, 2, 64, 64, 256], P('segment', None, 'dp'), may hold values from -0.75 to 0.75
- w_out: bfloat16 [4, 2, 64, 64, 256], P('segment', None, 'dp'), may hold values from -0.375 to 0.375
- gains: bfloat16 [4, 2, 4096], P('segment', None, 'dp'), may hold values from 0.25 to 1.75
- counts: int32 [4], replicated, may hold values from 1 to 2, 6 in all
Outputs:
- segment_out: bfloat16 [4, 2, 512, 4096], P('segment', None, 'dp')
- segment_grad: bfloat16 [4, 2, 512, 4096], P('segment', None, 'dp')
- grad_in: float32 [4, 2, 64, 64, 256], P('segment', None, 'dp')
- grad_out: float32 [4, 2, 64, 64, 256], P('segment', None, 'dp')
- grad_gain: float32 [4, 2, 4096], P('segment', None, 'dp')
The draws below stay inside these ranges and needn't reach their ends.
All inputs are finite; a program needn't handle non-finite values.
Results may differ from the reference program's by a relative error of at most 0.023.
Values may be sent and summed in bfloat16 or wider, within the bound.
A program may use at most 192 MiB of HBM per device.

```python
import math
import jax
import jax.numpy as jnp
import numpy as np
from jax import lax

NB = 64
BI = 64
BO = 256
LCAP = 2
MB = 2
TOK_DEV = 64
D = 4096
LAYERS = 6
TOKENS = 512
N_SEGMENT = 4
N_DP = 8


def shard_levels(key, dims, shards, least, high):
    level, own = 1.0, jax.random.fold_in(key, 6)
    for dim, shards_of in shards:
        heights = jnp.exp(jax.random.uniform(jax.random.fold_in(own, dim), (shards_of,), jnp.float32, least / len(shards), high / len(shards)))
        level = level * jnp.repeat(heights, dims[dim] // shards_of).reshape([-1 if axis == dim else 1 for axis in range(len(dims))])
    return level


def length_profile(number_of, total, most, skew):
    portions = [(1 << 20) // math.isqrt(standing ** skew) + 1 for standing in range(2, number_of + 1)]
    spare, given = total - most - (number_of - 1), [1] * (number_of - 1)
    while spare > 0:
        free = [i for i in range(number_of - 1) if given[i] < most]
        pool, budget = sum([portions[i] for i in free]), spare
        for i in free:
            more = min(most - given[i], max(1, budget * portions[i] // pool), spare)
            given[i] = given[i] + more
            spare = spare - more
    return np.array([most] + given)


def uneven_parts(rng, count, total, reach, skew):
    if count == 2:
        one = jax.random.randint(rng, (), max(1, total - reach), min(reach, total - 1) + 1)
        return jnp.stack([one, total - one])
    sizes = jnp.asarray(length_profile(count, total, reach, skew), jnp.int32)
    twos = (count - 1) // 2
    giver, taker = sizes[1:1 + 2 * twos:2], sizes[2:2 + 2 * twos:2]
    room = jnp.minimum(giver - 1, reach - taker)
    passed = jax.random.randint(jax.random.fold_in(rng, 1), (twos,), 0, 1 << 20) % (room + 1)
    sizes = sizes.at[1:1 + 2 * twos:2].set(giver - passed).at[2:2 + 2 * twos:2].set(taker + passed)
    return sizes[jax.random.permutation(jax.random.fold_in(rng, 2), count)]


def scatter_about(rng, shape, scale, bound, shards=(), kind=jnp.bfloat16):
    result = jax.random.normal(rng, shape, jnp.float32) * scale
    if len(shards) > 0:
        result = shard_levels(rng, shape, shards, -0.22, 0.18) * result
    return jnp.clip(result, min=-bound, max=bound).astype(kind)


def setup_inputs(seed: int = 0) -> dict:
    streams_of = jax.random.split(jax.random.key(seed), 7)
    inputs = scatter_about(streams_of[0], (MB, TOKENS, D), 1.0, 6.0, ((1, 8),))
    cotangent = scatter_about(streams_of[1], (MB, TOKENS, D), 0.25, 2.0, ((1, 8),))
    w_in = scatter_about(streams_of[2], (N_SEGMENT, LCAP, NB, BI, BO), BI ** -0.5, 0.75, ((0, 4), (2, 8)))
    w_out = scatter_about(streams_of[3], (N_SEGMENT, LCAP, NB, BI, BO), BO ** -0.5, 0.375, ((0, 4), (2, 8)))
    gains = jnp.clip(1.0 + 0.15 * jax.random.normal(streams_of[4], (N_SEGMENT, LCAP, D), jnp.float32), 0.25, 1.75).astype(jnp.bfloat16)
    counts = uneven_parts(streams_of[5], N_SEGMENT, LAYERS, LCAP, 0).astype(jnp.int32)
    return dict(inputs=inputs, cotangent=cotangent, w_in=w_in, w_out=w_out, gains=gains, counts=counts)


def layer(stream, weight_in, weight_out, gain_row):
    row_count = stream.shape[0]
    block_count = weight_in.shape[0]
    block_out = weight_in.shape[2]
    widened = stream.astype(jnp.float32)
    mean_square = lax.optimization_barrier(jnp.mean(widened * widened, axis=-1, keepdims=True))
    normed = (widened * lax.rsqrt(mean_square + 1e-05) * gain_row).astype(jnp.bfloat16)
    blocks = normed.reshape(row_count, block_count, weight_in.shape[1]).astype(jnp.float32)
    hidden = jnp.einsum('tbi,bio->tbo', blocks, weight_in.astype(jnp.float32))
    permuted = jnp.transpose(hidden, (0, 2, 1)).reshape(row_count, block_count, block_out)
    active = jax.nn.gelu(permuted, approximate=True).astype(jnp.bfloat16)
    update = jnp.einsum('tbo,bio->tbi', active.astype(jnp.float32), weight_out.astype(jnp.float32))
    return (widened + update.reshape(row_count, -1)).astype(jnp.bfloat16)

def reduce_replicas(per_replica):
    grouped = per_replica.reshape((MB, N_DP) + per_replica.shape[1:]).astype(jnp.float32)
    partial_sum = lax.optimization_barrier(jnp.sum(grouped, axis=0))
    rounded = lax.optimization_barrier(partial_sum.astype(jnp.bfloat16)).astype(jnp.float32)
    return lax.optimization_barrier(jnp.sum(rounded, axis=0))

def reference(inputs, cotangent, w_in, w_out, gains, counts):
    replicas = MB * N_DP
    stream = inputs.reshape(replicas, TOK_DEV, D)
    saved = []
    outputs = []
    for segment in range(N_SEGMENT):
        for slot in range(LCAP):
            saved.append(stream)
            moved = jax.vmap(layer, in_axes=(0, None, None, None))(stream, w_in[segment, slot], w_out[segment, slot], gains[segment, slot])
            stream = jnp.where(slot < counts[segment], moved, stream)
        outputs.append(stream.reshape(MB, TOKENS, D))
    segment_out = jnp.stack(outputs)
    upstream = cotangent.reshape(replicas, TOK_DEV, D)
    grads_in = [[None] * LCAP for segment in range(N_SEGMENT)]
    grads_out = [[None] * LCAP for segment in range(N_SEGMENT)]
    grads_gain = [[None] * LCAP for segment in range(N_SEGMENT)]
    back_list = [None] * N_SEGMENT
    for segment in reversed(range(N_SEGMENT)):
        for slot in reversed(range(LCAP)):

            def pull_one(stream_in, grad_in_row, segment=segment, slot=slot):
                unused, pullback = jax.vjp(layer, stream_in, w_in[segment, slot], w_out[segment, slot], gains[segment, slot])
                return pullback(grad_in_row)
            down, first_grad, second_grad, gain_grad = jax.vmap(pull_one)(saved[segment * LCAP + slot], upstream)
            live = slot < counts[segment]
            upstream = jnp.where(live, down, upstream)
            grads_in[segment][slot] = jnp.where(live, reduce_replicas(first_grad), 0.0)
            grads_out[segment][slot] = jnp.where(live, reduce_replicas(second_grad), 0.0)
            grads_gain[segment][slot] = jnp.where(live, reduce_replicas(gain_grad), 0.0)
        back_list[segment] = upstream.reshape(MB, TOKENS, D)
    segment_grad = jnp.stack(back_list)
    grad_in = jnp.stack([jnp.stack(row) for row in grads_in])
    grad_out = jnp.stack([jnp.stack(row) for row in grads_out])
    grad_gain = jnp.stack([jnp.stack(row) for row in grads_gain])
    return (segment_out, segment_grad, grad_in, grad_out, grad_gain)
```

```python
from functools import partial

import jax
import jax.numpy as jnp
from jax import lax
from jax.experimental import pallas as pl
from jax.experimental.pallas import tpu as pltpu
from jax.sharding import PartitionSpec as P

EPS = 1e-05
GROUP = 8
VMEM_BYTES = 48 * 1024 * 1024
C0 = 0.7978845608028654
C1 = 0.044715


def dot_tn(a, b):
    return lax.dot_general(a, b, (((0,), (0,)), ((), ())), preferred_element_type=jnp.float32)


def dot_nt(a, b):
    return lax.dot_general(a, b, (((1,), (1,)), ((), ())), preferred_element_type=jnp.float32)


def dot_nn(a, b):
    return lax.dot_general(a, b, (((1,), (0,)), ((), ())), preferred_element_type=jnp.float32)


def inverse_rms(x_ref, chunk):
    width, tokens = x_ref.shape

    def add(i, total):
        x = x_ref[pl.ds(pl.multiple_of(i * chunk, chunk), chunk), :].astype(jnp.float32)
        return total + jnp.sum((x * x).reshape(chunk // 8, 8, tokens), axis=0)

    total = lax.fori_loop(0, width // chunk, add, jnp.zeros((8, tokens), jnp.float32), unroll=4)
    mean = jnp.sum(total, axis=0, keepdims=True) / width
    return lax.rsqrt(mean + EPS)


def forward_kernel(x_ref, w_in_ref, w_out_ref, gain_ref, y_ref, act_ref, slope_ref, hid_ref, r_ref):
    step = pl.program_id(0)
    steps = pl.num_programs(0) // 2
    group, bi, bo = w_in_ref.shape
    nb = group * steps

    @pl.when(step == 0)
    def _():
        r_ref[...] = jnp.broadcast_to(inverse_rms(x_ref, bi), r_ref.shape)

    @pl.when(step < steps)
    def _():
        r = r_ref[0:1, :]
        for k in range(group):
            b = step * group + k
            rows = pl.ds(pl.multiple_of(b * bi, bi), bi)
            x = x_ref[rows, :].astype(jnp.float32)
            normed = (x * r * gain_ref[rows, :].astype(jnp.float32)).astype(jnp.bfloat16)
            hid_ref[pl.ds(b, bo, stride=nb), :] = dot_tn(w_in_ref[k], normed)

    @pl.when(step >= steps)
    def _():
        for k in range(group):
            b = (step - steps) * group + k
            rows = pl.ds(pl.multiple_of(b * bi, bi), bi)
            h = hid_ref[pl.ds(pl.multiple_of(b * bo, bo), bo), :]
            sq = h * h
            th = jnp.tanh(C0 * h * (1.0 + C1 * sq))
            half = 0.5 * (1.0 + th)
            act = (h * half).astype(jnp.bfloat16)
            slope = half + 0.5 * h * (1.0 - th * th) * (C0 * (1.0 + 3.0 * C1 * sq))
            own = pl.ds(k * bo, bo)
            act_ref[own, :] = act
            slope_ref[own, :] = slope.astype(jnp.bfloat16)
            v = dot_nn(w_out_ref[k], act)
            y_ref[rows, :] = (x_ref[rows, :].astype(jnp.float32) + v).astype(jnp.bfloat16)


def backward_kernel(
    x_ref, g_ref, w_in_ref, w_out_ref, gain_ref, act_ref, slope_ref,
    dx_ref, d_in_ref, d_out_ref, d_gain_ref, hid_ref, q_ref, r_ref, s_ref,
):
    step = pl.program_id(0)
    steps = pl.num_programs(0) // 2
    group, bi, bo = w_in_ref.shape
    nb = group * steps

    @pl.when(step == 0)
    def _():
        r_ref[...] = jnp.broadcast_to(inverse_rms(x_ref, bi), r_ref.shape)
        s_ref[...] = jnp.zeros_like(s_ref)

    @pl.when(step < steps)
    def _():
        for k in range(group):
            b = step * group + k
            g = g_ref[pl.ds(pl.multiple_of(b * bi, bi), bi), :]
            own = pl.ds(k * bo, bo)
            d_act = dot_tn(w_out_ref[k], g)
            hid_ref[pl.ds(pl.multiple_of(b * bo, bo), bo), :] = d_act * slope_ref[own, :].astype(
                jnp.float32
            )
            d_out_ref[k] = dot_nt(g, act_ref[own, :]).astype(jnp.bfloat16)

    @pl.when(step >= steps)
    def _():
        r = r_ref[0:1, :]
        for k in range(group):
            b = (step - steps) * group + k
            rows = pl.ds(pl.multiple_of(b * bi, bi), bi)
            d_hid = hid_ref[pl.ds(b, bo, stride=nb), :].astype(jnp.bfloat16)
            d_norm = dot_nn(w_in_ref[k], d_hid)
            x = x_ref[rows, :].astype(jnp.float32)
            gain = gain_ref[rows, :].astype(jnp.float32)
            unit = x * r
            normed = (unit * gain).astype(jnp.bfloat16)
            d_in_ref[k] = dot_nt(normed, d_hid).astype(jnp.bfloat16)
            d_gain_ref[rows, :] = jnp.sum(d_norm * unit, axis=1, keepdims=True)
            q = d_norm * gain
            q_ref[rows, :] = q
            s_ref[...] += jnp.sum((q * x).reshape(bi // 8, 8, q.shape[1]), axis=0)

    @pl.when(step == 2 * steps - 1)
    def _():
        width = x_ref.shape[0]
        r = r_ref[0:1, :]
        s = jnp.sum(s_ref[...], axis=0, keepdims=True) * (r * r * r) / width

        def finish(i, carry):
            rows = pl.ds(pl.multiple_of(i * bi, bi), bi)
            x = x_ref[rows, :].astype(jnp.float32)
            g = g_ref[rows, :].astype(jnp.float32)
            dx_ref[rows, :] = (g + (q_ref[rows, :] * r - x * s)).astype(jnp.bfloat16)
            return carry

        lax.fori_loop(0, width // bi, finish, 0, unroll=4)


def whole(shape):
    return pl.BlockSpec(shape, lambda i: (0,) * len(shape))


def forward_layer(x, w_in, w_out, gain):
    width, tokens = x.shape
    nb, bi, bo = w_in.shape
    group = min(GROUP, nb)
    steps = nb // group
    first = lambda i: (jnp.minimum(i, steps - 1), 0, 0)
    second = lambda i: (jnp.maximum(i - steps, 0), 0, 0)
    second2 = lambda i: (jnp.maximum(i - steps, 0), 0)
    return pl.pallas_call(
        forward_kernel,
        grid=(2 * steps,),
        out_shape=(
            jax.ShapeDtypeStruct((width, tokens), jnp.bfloat16),
            jax.ShapeDtypeStruct((nb * bo, tokens), jnp.bfloat16),
            jax.ShapeDtypeStruct((nb * bo, tokens), jnp.bfloat16),
        ),
        in_specs=[
            whole((width, tokens)),
            pl.BlockSpec((group, bi, bo), first),
            pl.BlockSpec((group, bi, bo), second),
            whole((width, tokens)),
        ],
        out_specs=(
            whole((width, tokens)),
            pl.BlockSpec((group * bo, tokens), second2),
            pl.BlockSpec((group * bo, tokens), second2),
        ),
        scratch_shapes=[
            pltpu.VMEM((nb * bo, tokens), jnp.float32),
            pltpu.VMEM((8, tokens), jnp.float32),
        ],
        compiler_params=pltpu.CompilerParams(vmem_limit_bytes=VMEM_BYTES),
        name="layer_forward",
    )(x, w_in, w_out, gain)


def backward_layer(x, g, w_in, w_out, gain, act, slope):
    width, tokens = x.shape
    nb, bi, bo = w_in.shape
    group = min(GROUP, nb)
    steps = nb // group
    first = lambda i: (jnp.minimum(i, steps - 1), 0, 0)
    first2 = lambda i: (jnp.minimum(i, steps - 1), 0)
    second = lambda i: (jnp.maximum(i - steps, 0), 0, 0)
    weight = jax.ShapeDtypeStruct((nb, bi, bo), jnp.bfloat16)
    return pl.pallas_call(
        backward_kernel,
        grid=(2 * steps,),
        out_shape=(
            jax.ShapeDtypeStruct((width, tokens), jnp.bfloat16),
            weight,
            weight,
            jax.ShapeDtypeStruct((width, 1), jnp.float32),
        ),
        in_specs=[
            whole((width, tokens)),
            whole((width, tokens)),
            pl.BlockSpec((group, bi, bo), second),
            pl.BlockSpec((group, bi, bo), first),
            whole((width, tokens)),
            pl.BlockSpec((group * bo, tokens), first2),
            pl.BlockSpec((group * bo, tokens), first2),
        ],
        out_specs=(
            whole((width, tokens)),
            pl.BlockSpec((group, bi, bo), second),
            pl.BlockSpec((group, bi, bo), first),
            whole((width, 1)),
        ),
        scratch_shapes=[
            pltpu.VMEM((nb * bo, tokens), jnp.float32),
            pltpu.VMEM((width, tokens), jnp.float32),
            pltpu.VMEM((8, tokens), jnp.float32),
            pltpu.VMEM((8, tokens), jnp.float32),
        ],
        compiler_params=pltpu.CompilerParams(vmem_limit_bytes=VMEM_BYTES),
        name="layer_backward",
    )(x, g, w_in, w_out, gain, act, slope)


def to_columns(a):
    micro, rows, width = a.shape
    return a.reshape(micro * rows, width).T


def per_device(inputs, cotangent, w_in, w_out, gains, counts):
    segment_count = lax.axis_size("segment")
    my_segment = lax.axis_index("segment")
    slot_count = w_in.shape[1]
    micro, rows, width = inputs.shape
    tokens = micro * rows
    count_here = jnp.sum(jnp.where(jnp.arange(segment_count) == my_segment, counts, 0))
    full_in = [lax.all_gather(w_in[0, l], "dp", axis=0, tiled=True) for l in range(slot_count)]
    full_out = [lax.all_gather(w_out[0, l], "dp", axis=0, tiled=True) for l in range(slot_count)]
    full_gain = lax.all_gather(gains[0], "dp", axis=1, tiled=True)
    gain = [
        jnp.broadcast_to(full_gain[l][:, None], (width, tokens)) for l in range(slot_count)
    ]
    nb, bi, bo = full_in[0].shape
    first_x = to_columns(inputs)
    last_g = to_columns(cotangent)

    def run_forward(operands):
        x, saved = operands
        kept = []
        for l in range(slot_count):
            def live(x, l=l):
                return forward_layer(x, full_in[l], full_out[l], gain[l])

            if l == 0:
                y, act, slope = live(x)
            else:
                y, act, slope = lax.cond(
                    l < count_here, live, lambda x, l=l: (x, saved[l][1], saved[l][2]), x
                )
            kept.append((x, act, slope))
            x = y
        return x, tuple(kept)

    def keep(operands):
        return operands

    hid = jnp.zeros((nb * bo, tokens), jnp.bfloat16)
    saved = tuple((first_x, hid, hid) for l in range(slot_count))
    x = first_x
    result = x
    for k in range(segment_count):
        x, saved = lax.cond(my_segment == k, run_forward, keep, (x, saved))
        result = jnp.where(my_segment == k, x, result)
        if k < segment_count - 1:
            x = lax.ppermute(x, "segment", [(k, k + 1)])

    def run_backward(operands):
        g, grads = operands
        out = [None] * slot_count
        for l in reversed(range(slot_count)):
            x, act, slope = saved[l]

            def live(g, l=l, x=x, act=act, slope=slope):
                return backward_layer(x, g, full_in[l], full_out[l], gain[l], act, slope)

            if l == 0:
                g, *out[l] = live(g)
            else:
                g, *out[l] = lax.cond(l < count_here, live, lambda g, l=l: (g, *grads[l]), g)
        return g, tuple(tuple(o) for o in out)

    zero_weight = jnp.zeros((nb, bi, bo), jnp.bfloat16)
    zero_gain = jnp.zeros((width, 1), jnp.float32)
    grads = tuple((zero_weight, zero_weight, zero_gain) for l in range(slot_count))
    g = last_g
    down = g
    for k in reversed(range(segment_count)):
        g, grads = lax.cond(my_segment == k, run_backward, keep, (g, grads))
        down = jnp.where(my_segment == k, g, down)
        if k > 0:
            g = lax.ppermute(g, "segment", [(k, k - 1)])

    def scatter(a):
        return lax.psum_scatter(
            a.astype(jnp.bfloat16), "dp", scatter_dimension=0, tiled=True
        ).astype(jnp.float32)

    grad_in = jnp.stack([scatter(grads[l][0]) for l in range(slot_count)])[None]
    grad_out = jnp.stack([scatter(grads[l][1]) for l in range(slot_count)])[None]
    all_gain = jnp.stack([grads[l][2][:, 0] for l in range(slot_count)], axis=1)
    grad_gain = scatter(all_gain).T[None]
    outputs = result.T.reshape(1, micro, rows, width)
    grads_kept = down.T.reshape(1, micro, rows, width)
    return outputs, grads_kept, grad_in, grad_out, grad_gain


def solution(mesh):
    in_specs = (
        P(None, "dp", None),
        P(None, "dp", None),
        P("segment", None, "dp", None, None),
        P("segment", None, "dp", None, None),
        P("segment", None, "dp"),
        P(),
    )
    out_specs = (
        P("segment", None, "dp", None),
        P("segment", None, "dp", None),
        P("segment", None, "dp", None, None),
        P("segment", None, "dp", None, None),
        P("segment", None, "dp"),
    )
    return jax.shard_map(
        per_device, mesh=mesh, in_specs=in_specs, out_specs=out_specs, check_vma=False
    )
```

```python
from functools import partial

import jax
import jax.numpy as jnp
from jax import lax
from jax.experimental import pallas as pl
from jax.experimental.pallas import tpu as pltpu
from jax.sharding import PartitionSpec as P

EPS = 1e-05
GROUP = 8
VMEM_BYTES = 48 * 1024 * 1024
C0 = 0.7978845608028654
C1 = 0.044715


def dot_tn(a, b):
    return lax.dot_general(a, b, (((0,), (0,)), ((), ())), preferred_element_type=jnp.float32)


def dot_nt(a, b):
    return lax.dot_general(a, b, (((1,), (1,)), ((), ())), preferred_element_type=jnp.float32)


def dot_nn(a, b):
    return lax.dot_general(a, b, (((1,), (0,)), ((), ())), preferred_element_type=jnp.float32)


def inverse_rms(x_ref, chunk):
    width, tokens = x_ref.shape

    def add(i, total):
        x = x_ref[pl.ds(pl.multiple_of(i * chunk, chunk), chunk), :].astype(jnp.float32)
        return total + jnp.sum((x * x).reshape(chunk // 8, 8, tokens), axis=0)

    total = lax.fori_loop(0, width // chunk, add, jnp.zeros((8, tokens), jnp.float32), unroll=4)
    mean = jnp.sum(total, axis=0, keepdims=True) / width
    return lax.rsqrt(mean + EPS)


def forward_kernel(x_ref, w_in_ref, w_out_ref, gain_ref, y_ref, act_ref, slope_ref, hid_ref, r_ref):
    step = pl.program_id(0)
    steps = pl.num_programs(0) // 2
    group, bi, bo = w_out_ref.shape
    nb = group * steps

    @pl.when(step == 0)
    def _():
        r_ref[...] = jnp.broadcast_to(inverse_rms(x_ref, bi), r_ref.shape)

    @pl.when(step < steps)
    def _():
        r = r_ref[0:1, :]
        for k in range(group):
            b = step * group + k
            rows = pl.ds(pl.multiple_of(b * bi, bi), bi)
            x = x_ref[rows, :].astype(jnp.float32)
            normed = (x * r * gain_ref[rows, :].astype(jnp.float32)).astype(jnp.bfloat16)
            hid_ref[pl.ds(b, bo, stride=nb), :] = dot_tn(w_in_ref[k, :bi, :], normed)

    @pl.when(step >= steps)
    def _():
        for k in range(group):
            b = (step - steps) * group + k
            rows = pl.ds(pl.multiple_of(b * bi, bi), bi)
            h = hid_ref[pl.ds(pl.multiple_of(b * bo, bo), bo), :]
            sq = h * h
            th = jnp.tanh(C0 * h * (1.0 + C1 * sq))
            half = 0.5 * (1.0 + th)
            act = (h * half).astype(jnp.bfloat16)
            slope = half + 0.5 * h * (1.0 - th * th) * (C0 * (1.0 + 3.0 * C1 * sq))
            own = pl.ds(k * bo, bo)
            act_ref[own, :] = act
            slope_ref[own, :] = slope.astype(jnp.bfloat16)
            v = dot_nn(w_out_ref[k], act)
            y_ref[rows, :] = (x_ref[rows, :].astype(jnp.float32) + v).astype(jnp.bfloat16)


def backward_kernel(
    x_ref, g_ref, w_in_ref, w_out_ref, gain_ref, act_ref, slope_ref,
    dx_ref, d_in_ref, d_out_ref, hid_ref, q_ref, r_ref, s_ref,
):
    step = pl.program_id(0)
    steps = pl.num_programs(0) // 2
    group, bi, bo = w_out_ref.shape
    nb = group * steps

    @pl.when(step == 0)
    def _():
        r_ref[...] = jnp.broadcast_to(inverse_rms(x_ref, bi), r_ref.shape)
        s_ref[...] = jnp.zeros_like(s_ref)

    @pl.when(step < steps)
    def _():
        for k in range(group):
            b = step * group + k
            g = g_ref[pl.ds(pl.multiple_of(b * bi, bi), bi), :]
            own = pl.ds(k * bo, bo)
            d_act = dot_tn(w_out_ref[k], g)
            hid_ref[pl.ds(pl.multiple_of(b * bo, bo), bo), :] = d_act * slope_ref[own, :].astype(
                jnp.float32
            )
            d_out_ref[k] = dot_nt(g, act_ref[own, :]).astype(jnp.bfloat16)

    @pl.when(step >= steps)
    def _():
        r = r_ref[0:1, :]
        for k in range(group):
            b = (step - steps) * group + k
            rows = pl.ds(pl.multiple_of(b * bi, bi), bi)
            d_hid = hid_ref[pl.ds(b, bo, stride=nb), :].astype(jnp.bfloat16)
            d_norm = dot_nn(w_in_ref[k, :bi, :], d_hid)
            x = x_ref[rows, :].astype(jnp.float32)
            gain = gain_ref[rows, :].astype(jnp.float32)
            unit = x * r
            normed = (unit * gain).astype(jnp.bfloat16)
            d_in_ref[k, :bi, :] = dot_nt(normed, d_hid).astype(jnp.bfloat16)
            extra = d_in_ref.shape[1] - bi
            ones = jnp.ones((extra, x.shape[1]), jnp.bfloat16)
            d_gain = dot_nt(ones, (d_norm * unit).astype(jnp.bfloat16))
            d_in_ref[k, bi:, :] = jnp.concatenate(
                [d_gain, jnp.zeros((extra, bo - bi), jnp.float32)], axis=1
            ).astype(jnp.bfloat16)
            q = d_norm * gain
            q_ref[rows, :] = q
            s_ref[...] += jnp.sum((q * x).reshape(bi // 8, 8, q.shape[1]), axis=0)

    @pl.when(step == 2 * steps - 1)
    def _():
        width = x_ref.shape[0]
        r = r_ref[0:1, :]
        s = jnp.sum(s_ref[...], axis=0, keepdims=True) * (r * r * r) / width

        def finish(i, carry):
            rows = pl.ds(pl.multiple_of(i * bi, bi), bi)
            x = x_ref[rows, :].astype(jnp.float32)
            g = g_ref[rows, :].astype(jnp.float32)
            dx_ref[rows, :] = (g + (q_ref[rows, :] * r - x * s)).astype(jnp.bfloat16)
            return carry

        lax.fori_loop(0, width // bi, finish, 0, unroll=4)


MESH = pl.DeviceIdType.MESH


def grid_of(dp):
    x = 1
    while 2 * (2 * x) * (2 * x) <= dp and dp % (2 * x) == 0:
        x = 2 * x
    return dp // x, x


class Place:
    def __init__(self, zs, xs):
        self.zs, self.xs = zs, xs
        self.segment = lax.axis_index("segment")
        self.me = lax.axis_index("dp")
        self.z, self.x = self.me // xs, self.me % xs

    def at(self, z, x):
        return (self.segment, z * self.xs + x)

    def beside(self, j):
        return lax.rem(self.x + j, self.xs)

    def enter(self):
        barrier = pltpu.get_barrier_semaphore()

        def greet(z, x):
            pl.semaphore_signal(barrier, inc=1, device_id=self.at(z, x), device_id_type=MESH)

        for j in range(1, self.xs):
            greet(self.z, self.beside(j))

        @pl.when(self.z > 0)
        def _():
            greet(self.z - 1, self.x)

        @pl.when(self.z < self.zs - 1)
        def _():
            greet(self.z + 1, self.x)

        count = self.xs - 1 + jnp.where(self.z > 0, 1, 0) + jnp.where(self.z < self.zs - 1, 1, 0)
        pl.semaphore_wait(barrier, count)

    def copy(self, src, dst, send, recv, z, x):
        return pltpu.make_async_remote_copy(
            src_ref=src, dst_ref=dst, send_sem=send, recv_sem=recv,
            device_id=self.at(z, x), device_id_type=MESH,
        )


def gather_kernel(
    zs, xs, a_ref, b_ref, ga_ref, gb_ref,
    own_sem, ax_send, ax_recv, bx_send, bx_recv, az_send, az_recv, bz_send, bz_recv,
):
    place = Place(zs, xs)
    z, x = place.z, place.x
    slots = a_ref.shape[0]
    place.enter()

    def own(l, which):
        src, dst = (a_ref, ga_ref) if which == 0 else (b_ref, gb_ref)
        return pltpu.make_async_copy(src.at[l], dst.at[l, z, x], own_sem.at[l, which])

    def a_beside(l, j, from_x):
        return place.copy(
            a_ref.at[l], ga_ref.at[l, z, from_x], ax_send.at[l, j], ax_recv.at[l, j],
            z, place.beside(j),
        )

    def b_beside(l, row, j, from_x):
        return place.copy(
            gb_ref.at[l, row, from_x], gb_ref.at[l, row, from_x],
            bx_send.at[l, row, j], bx_recv.at[l, row, j], z, place.beside(j),
        )

    def line(which, l, way, step, row, to_z):
        if which == 0:
            ref, send, recv = ga_ref.at[l, row], az_send, az_recv
        else:
            ref, send, recv = gb_ref.at[l, row, x], bz_send, bz_recv
        return place.copy(ref, ref, send.at[l, way, step], recv.at[l, way, step], to_z, x)

    def sends(which, l, step, act):
        @pl.when((z - step >= 0) & (z + 1 < zs))
        def _():
            act(line(which, l, 0, step, z - step, z + 1))

        @pl.when((z + step < zs) & (z - 1 >= 0))
        def _():
            act(line(which, l, 1, step, z + step, z - 1))

    def receives(which, l, step, then):
        @pl.when(z - 1 - step >= 0)
        def _():
            line(which, l, 0, step, z - 1 - step, z).wait_recv()
            then(z - 1 - step)

        @pl.when(z + 1 + step < zs)
        def _():
            line(which, l, 1, step, z + 1 + step, z).wait_recv()
            then(z + 1 + step)

    def begin(c):
        c.start()

    def done(c):
        c.wait_send()

    def spread(l, row):
        for j in range(1, xs):
            b_beside(l, row, j, x).start()

    for l in range(slots):
        own(l, 0).start()
        own(l, 1).start()
        for j in range(1, xs):
            a_beside(l, j, x).start()
    for l in range(slots):
        own(l, 1).wait()
        sends(1, l, 0, begin)
        spread(l, z)
    for l in range(slots):
        own(l, 0).wait()
        for j in range(1, xs):
            a_beside(l, j, lax.rem(x + xs - j, xs)).wait_recv()
        sends(0, l, 0, begin)
    for step in range(zs - 1):
        for l in range(slots):
            for which in (1, 0):
                receives(which, l, step, partial(spread, l) if which == 1 else lambda row: None)
                if step < zs - 2:
                    sends(which, l, step + 1, begin)
    for l in range(slots):
        for j in range(1, xs):
            a_beside(l, j, x).wait_send()
            for row in range(zs):
                b_beside(l, row, j, lax.rem(x + xs - j, xs)).wait_recv()
                b_beside(l, row, j, x).wait_send()
        for which in (0, 1):
            for step in range(zs - 1):
                sends(which, l, step, done)


def gather_weights(a, b, dp):
    zs, xs = grid_of(dp)
    slots = a.shape[0]
    dma = pltpu.SemaphoreType.DMA
    ga, gb = pl.pallas_call(
        partial(gather_kernel, zs, xs),
        out_shape=tuple(
            jax.ShapeDtypeStruct((slots, zs, xs) + w.shape[1:], w.dtype) for w in (a, b)
        ),
        in_specs=[pl.BlockSpec(memory_space=pl.ANY)] * 2,
        out_specs=(pl.BlockSpec(memory_space=pl.ANY),) * 2,
        scratch_shapes=[dma((slots, 2)), dma((slots, xs)), dma((slots, xs))]
        + [dma((slots, zs, xs))] * 2
        + [dma((slots, 2, zs))] * 4,
        compiler_params=pltpu.CompilerParams(
            collective_id=0, has_side_effects=True, vmem_limit_bytes=VMEM_BYTES
        ),
        name="gather_weights",
    )(a, b)
    return tuple(g.reshape((slots, -1) + g.shape[4:]) for g in (ga, gb))


def scatter_kernel(
    zs, xs, a_ref, b_ref, oa_ref, ob_ref,
    a_line, b_line, a_sum, a_side, b_col, b_side,
    ax_send, ax_recv, bx_send, bx_recv, az_send, az_recv, bz_send, bz_recv,
):
    place = Place(zs, xs)
    z, x = place.z, place.x
    slots, n = a_ref.shape[0], a_ref.shape[3]
    f32, bf16 = jnp.float32, jnp.bfloat16
    place.enter()

    def each(count, body):
        def step(i, carry):
            body(i)
            return carry

        lax.fori_loop(0, count, step, 0)

    def b_beside(l, j):
        return place.copy(
            b_ref.at[l, :, place.beside(j)], b_side.at[l, j], bx_send.at[l, j], bx_recv.at[l, j],
            z, place.beside(j),
        )

    def a_beside(l, j):
        return place.copy(
            a_sum.at[l, place.beside(j)], a_side.at[l, j], ax_send.at[l, j], ax_recv.at[l, j],
            z, place.beside(j),
        )

    def mine(which, l, row):
        return a_ref.at[l, row] if which == 0 else b_col.at[l, row]

    def line(which, l, way, step, src, to_z):
        buf, send, recv = (
            (a_line, az_send, az_recv) if which == 0 else (b_line, bz_send, bz_recv)
        )
        return place.copy(
            src, buf.at[l, way, step], send.at[l, way, step], recv.at[l, way, step], to_z, x
        )

    def row_of(way, step):
        return zs - 1 - step if way == 0 else step

    def advance(which, l, way, step):
        buf = (a_line if which == 0 else b_line).at[l, way, step]
        row = row_of(way, step)
        own = mine(which, l, row)
        to_z = z + 1 if way == 0 else z - 1
        first = z == 0 if way == 0 else z == zs - 1
        beyond = z < row if way == 0 else z > row
        ahead = z <= row if way == 0 else z >= row

        @pl.when(jnp.logical_not(first) & ahead)
        def _():
            line(which, l, way, step, buf, z).wait_recv()

        @pl.when(jnp.logical_not(first) & beyond)
        def _():
            def add(i):
                at = (i // n, i % n) if which == 0 else (i,)
                buf[at] = (buf[at].astype(f32) + own[at].astype(f32)).astype(bf16)

            each(xs * n if which == 0 else n, add)
            line(which, l, way, step, buf, to_z).start()

        @pl.when(first & beyond)
        def _():
            line(which, l, way, step, own, to_z).start()

    def finish_sends(which, l, way, step):
        row = row_of(way, step)

        @pl.when(z < row if way == 0 else z > row)
        def _():
            buf = (a_line if which == 0 else b_line).at[l, way, step]
            line(which, l, way, step, buf, z + 1 if way == 0 else z - 1).wait_send()

    for l in reversed(range(slots)):
        for j in range(1, xs):
            b_beside(l, j).start()
    for l in reversed(range(slots)):
        for way in (0, 1):
            advance(0, l, way, 0)
    for l in reversed(range(slots)):
        for j in range(1, xs):
            b_beside(l, j).wait_recv()

        def column(i, l=l):
            row, k = i // n, i % n
            value = b_ref[l, row, x, k].astype(f32)
            for j in range(1, xs):
                value += b_side[l, j, row, k].astype(f32)
            b_col[l, row, k] = value.astype(bf16)

        each(zs * n, column)
        for way in (0, 1):
            advance(1, l, way, 0)
    for step in range(1, zs - 1):
        for l in reversed(range(slots)):
            for which in (0, 1):
                for way in (0, 1):
                    advance(which, l, way, step)

    for l in reversed(range(slots)):
        right, left = jnp.clip(zs - 1 - z, 0, zs - 2), jnp.clip(z, 0, zs - 2)
        has_right, has_left = z > 0, z < zs - 1

        def start_sum(i, l=l):
            p, k = i // n, i % n
            a_sum[l, p, k] = a_ref[l, z, p, k]

        def add_sum(way, at, i, l=l):
            p, k = i // n, i % n
            a_sum[l, p, k] = (
                a_sum[l, p, k].astype(f32) + a_line[l, way, at, p, k].astype(f32)
            ).astype(bf16)

        each(xs * n, start_sum)
        pl.when(has_right)(lambda: each(xs * n, partial(add_sum, 0, right)))
        pl.when(has_left)(lambda: each(xs * n, partial(add_sum, 1, left)))
        for j in range(1, xs):
            a_beside(l, j).start()

        def start_out(i, l=l):
            ob_ref[l, i] = b_col[l, z, i].astype(f32)

        def add_out(way, at, i, l=l):
            ob_ref[l, i] += b_line[l, way, at, i].astype(f32)

        each(n, start_out)
        pl.when(has_right)(lambda: each(n, partial(add_out, 0, right)))
        pl.when(has_left)(lambda: each(n, partial(add_out, 1, left)))
    for l in reversed(range(slots)):
        for j in range(1, xs):
            a_beside(l, j).wait_recv()

        def out(i, l=l):
            value = a_sum[l, x, i].astype(f32)
            for j in range(1, xs):
                value += a_side[l, j, i].astype(f32)
            oa_ref[l, i] = value

        each(n, out)
    for l in range(slots):
        for j in range(1, xs):
            a_beside(l, j).wait_send()
            b_beside(l, j).wait_send()
        for which in (0, 1):
            for way in (0, 1):
                for step in range(zs - 1):
                    finish_sends(which, l, way, step)


def scatter_grads(a, b, dp):
    zs, xs = grid_of(dp)
    slots, nb = a.shape[:2]
    n = nb // dp
    a, b = (g.reshape((slots, zs, xs, n) + g.shape[2:]) for g in (a, b))
    ta, tb = a.shape[4:], b.shape[4:]
    dma = pltpu.SemaphoreType.DMA
    bf16 = jnp.bfloat16
    vmem = pl.BlockSpec(memory_space=pltpu.VMEM)
    return pl.pallas_call(
        partial(scatter_kernel, zs, xs),
        out_shape=tuple(
            jax.ShapeDtypeStruct((slots, n) + t, jnp.float32) for t in (ta, tb)
        ),
        in_specs=[vmem, vmem],
        out_specs=(vmem, vmem),
        scratch_shapes=[
            pltpu.VMEM((slots, 2, zs - 1, xs, n) + ta, bf16),
            pltpu.VMEM((slots, 2, zs - 1, n) + tb, bf16),
            pltpu.VMEM((slots, xs, n) + ta, bf16),
            pltpu.VMEM((slots, xs, n) + ta, bf16),
            pltpu.VMEM((slots, zs, n) + tb, bf16),
            pltpu.VMEM((slots, xs, zs, n) + tb, bf16),
        ]
        + [dma((slots, xs))] * 4
        + [dma((slots, 2, zs))] * 4,
        compiler_params=pltpu.CompilerParams(
            collective_id=1, has_side_effects=True, vmem_limit_bytes=VMEM_BYTES
        ),
        name="scatter_grads",
    )(a, b)


def whole(shape):
    return pl.BlockSpec(shape, lambda i: (0,) * len(shape))


def forward_layer(x, w_in, w_out, gain):
    width, tokens = x.shape
    nb, bi, bo = w_out.shape
    wide = w_in.shape[1]
    group = min(GROUP, nb)
    steps = nb // group
    first = lambda i: (jnp.minimum(i, steps - 1), 0, 0)
    second = lambda i: (jnp.maximum(i - steps, 0), 0, 0)
    second2 = lambda i: (jnp.maximum(i - steps, 0), 0)
    return pl.pallas_call(
        forward_kernel,
        grid=(2 * steps,),
        out_shape=(
            jax.ShapeDtypeStruct((width, tokens), jnp.bfloat16),
            jax.ShapeDtypeStruct((nb * bo, tokens), jnp.bfloat16),
            jax.ShapeDtypeStruct((nb * bo, tokens), jnp.bfloat16),
        ),
        in_specs=[
            whole((width, tokens)),
            pl.BlockSpec((group, wide, bo), first),
            pl.BlockSpec((group, bi, bo), second),
            whole((width, tokens)),
        ],
        out_specs=(
            whole((width, tokens)),
            pl.BlockSpec((group * bo, tokens), second2),
            pl.BlockSpec((group * bo, tokens), second2),
        ),
        scratch_shapes=[
            pltpu.VMEM((nb * bo, tokens), jnp.float32),
            pltpu.VMEM((8, tokens), jnp.float32),
        ],
        compiler_params=pltpu.CompilerParams(vmem_limit_bytes=VMEM_BYTES),
        name="layer_forward",
    )(x, w_in, w_out, gain)


def backward_layer(x, g, w_in, w_out, gain, act, slope):
    width, tokens = x.shape
    nb, bi, bo = w_out.shape
    wide = w_in.shape[1]
    group = min(GROUP, nb)
    steps = nb // group
    first = lambda i: (jnp.minimum(i, steps - 1), 0, 0)
    first2 = lambda i: (jnp.minimum(i, steps - 1), 0)
    second = lambda i: (jnp.maximum(i - steps, 0), 0, 0)
    return pl.pallas_call(
        backward_kernel,
        grid=(2 * steps,),
        out_shape=(
            jax.ShapeDtypeStruct((width, tokens), jnp.bfloat16),
            jax.ShapeDtypeStruct((nb, wide, bo), jnp.bfloat16),
            jax.ShapeDtypeStruct((nb, bi, bo), jnp.bfloat16),
        ),
        in_specs=[
            whole((width, tokens)),
            whole((width, tokens)),
            pl.BlockSpec((group, wide, bo), second),
            pl.BlockSpec((group, bi, bo), first),
            whole((width, tokens)),
            pl.BlockSpec((group * bo, tokens), first2),
            pl.BlockSpec((group * bo, tokens), first2),
        ],
        out_specs=(
            whole((width, tokens)),
            pl.BlockSpec((group, wide, bo), second),
            pl.BlockSpec((group, bi, bo), first),
        ),
        scratch_shapes=[
            pltpu.VMEM((nb * bo, tokens), jnp.float32),
            pltpu.VMEM((width, tokens), jnp.float32),
            pltpu.VMEM((8, tokens), jnp.float32),
            pltpu.VMEM((8, tokens), jnp.float32),
        ],
        compiler_params=pltpu.CompilerParams(vmem_limit_bytes=VMEM_BYTES),
        name="layer_backward",
    )(x, g, w_in, w_out, gain, act, slope)


def to_columns(a):
    micro, rows, width = a.shape
    return a.reshape(micro * rows, width).T


def per_device(inputs, cotangent, w_in, w_out, gains, counts):
    segment_count = lax.axis_size("segment")
    my_segment = lax.axis_index("segment")
    slot_count = w_in.shape[1]
    micro, rows, width = inputs.shape
    tokens = micro * rows
    count_here = jnp.sum(jnp.where(jnp.arange(segment_count) == my_segment, counts, 0))
    dp = lax.axis_size("dp")
    own_nb, bi, bo = w_in.shape[2:]
    nb = own_nb * dp
    extra = 16
    gain_rows = jnp.pad(
        gains.reshape(slot_count, own_nb, 1, bi), ((0, 0), (0, 0), (0, extra - 1), (0, bo - bi))
    )
    full_in, full_out = gather_weights(
        jnp.concatenate([w_in[0], gain_rows], axis=2), w_out[0], dp
    )
    gain = [
        jnp.broadcast_to(full_in[l, :, bi, :bi].reshape(width, 1), (width, tokens))
        for l in range(slot_count)
    ]
    first_x = to_columns(inputs)
    last_g = to_columns(cotangent)

    def run_forward(operands):
        x, saved = operands
        kept = []
        for l in range(slot_count):
            def live(x, l=l):
                return forward_layer(x, full_in[l], full_out[l], gain[l])

            if l == 0:
                y, act, slope = live(x)
            else:
                y, act, slope = lax.cond(
                    l < count_here, live, lambda x, l=l: (x, saved[l][1], saved[l][2]), x
                )
            kept.append((x, act, slope))
            x = y
        return x, tuple(kept)

    def keep(operands):
        return operands

    hid = jnp.zeros((nb * bo, tokens), jnp.bfloat16)
    saved = tuple((first_x, hid, hid) for l in range(slot_count))
    x = first_x
    result = x
    for k in range(segment_count):
        x, saved = lax.cond(my_segment == k, run_forward, keep, (x, saved))
        result = jnp.where(my_segment == k, x, result)
        if k < segment_count - 1:
            x = lax.ppermute(x, "segment", [(k, k + 1)])

    def run_backward(operands):
        g, grads = operands
        out = [None] * slot_count
        for l in reversed(range(slot_count)):
            x, act, slope = saved[l]

            def live(g, l=l, x=x, act=act, slope=slope):
                return backward_layer(x, g, full_in[l], full_out[l], gain[l], act, slope)

            if l == 0:
                g, *out[l] = live(g)
            else:
                g, *out[l] = lax.cond(l < count_here, live, lambda g, l=l: (g, *grads[l]), g)
        return g, tuple(tuple(o) for o in out)

    zero_in = jnp.zeros((nb, bi + extra, bo), jnp.bfloat16)
    zero_out = jnp.zeros((nb, bi, bo), jnp.bfloat16)
    grads = tuple((zero_in, zero_out) for l in range(slot_count))
    g = last_g
    down = g
    for k in reversed(range(segment_count)):
        g, grads = lax.cond(my_segment == k, run_backward, keep, (g, grads))
        down = jnp.where(my_segment == k, g, down)
        if k > 0:
            g = lax.ppermute(g, "segment", [(k, k - 1)])

    sum_in, sum_out = scatter_grads(
        jnp.stack([grads[l][0] for l in range(slot_count)]),
        jnp.stack([grads[l][1] for l in range(slot_count)]),
        dp,
    )
    grad_in = sum_in[None, :, :, :bi, :]
    grad_out = sum_out[None]
    grad_gain = sum_in[:, :, bi, :bi].reshape(1, slot_count, own_nb * bi)
    outputs = result.T.reshape(1, micro, rows, width)
    grads_kept = down.T.reshape(1, micro, rows, width)
    return outputs, grads_kept, grad_in, grad_out, grad_gain


def solution(mesh):
    in_specs = (
        P(None, "dp", None),
        P(None, "dp", None),
        P("segment", None, "dp", None, None),
        P("segment", None, "dp", None, None),
        P("segment", None, "dp"),
        P(),
    )
    out_specs = (
        P("segment", None, "dp", None),
        P("segment", None, "dp", None),
        P("segment", None, "dp", None, None),
        P("segment", None, "dp", None, None),
        P("segment", None, "dp"),
    )
    return jax.shard_map(
        per_device, mesh=mesh, in_specs=in_specs, out_specs=out_specs, check_vma=False
    )
```

```python
from functools import partial

import jax
import jax.numpy as jnp
from jax import lax
from jax.experimental import pallas as pl
from jax.experimental.pallas import tpu as pltpu
from jax.sharding import PartitionSpec as P

EPS = 1e-05
GROUP = 8
VMEM_BYTES = 48 * 1024 * 1024
C0 = 0.7978845608028654
C1 = 0.044715


def dot_tn(a, b):
    return lax.dot_general(a, b, (((0,), (0,)), ((), ())), preferred_element_type=jnp.float32)


def dot_nt(a, b):
    return lax.dot_general(a, b, (((1,), (1,)), ((), ())), preferred_element_type=jnp.float32)


def dot_nn(a, b):
    return lax.dot_general(a, b, (((1,), (0,)), ((), ())), preferred_element_type=jnp.float32)


def inverse_rms(x_ref, chunk):
    width, tokens = x_ref.shape

    def add(i, total):
        x = x_ref[pl.ds(pl.multiple_of(i * chunk, chunk), chunk), :].astype(jnp.float32)
        return total + jnp.sum((x * x).reshape(chunk // 8, 8, tokens), axis=0)

    total = lax.fori_loop(0, width // chunk, add, jnp.zeros((8, tokens), jnp.float32), unroll=4)
    mean = jnp.sum(total, axis=0, keepdims=True) / width
    return lax.rsqrt(mean + EPS)


def forward_kernel(x_ref, w_in_ref, w_out_ref, gain_ref, y_ref, act_ref, slope_ref, hid_ref, r_ref):
    step = pl.program_id(0)
    steps = pl.num_programs(0) // 2
    group, bi, bo = w_out_ref.shape
    nb = group * steps

    @pl.when(step == 0)
    def _():
        r_ref[...] = jnp.broadcast_to(inverse_rms(x_ref, bi), r_ref.shape)

    @pl.when(step < steps)
    def _():
        r = r_ref[0:1, :]
        for k in range(group):
            b = step * group + k
            rows = pl.ds(pl.multiple_of(b * bi, bi), bi)
            x = x_ref[rows, :].astype(jnp.float32)
            normed = (x * r * gain_ref[rows, :].astype(jnp.float32)).astype(jnp.bfloat16)
            hid_ref[pl.ds(b, bo, stride=nb), :] = dot_tn(w_in_ref[k, :bi, :], normed)

    @pl.when(step >= steps)
    def _():
        for k in range(group):
            b = (step - steps) * group + k
            rows = pl.ds(pl.multiple_of(b * bi, bi), bi)
            h = hid_ref[pl.ds(pl.multiple_of(b * bo, bo), bo), :]
            sq = h * h
            th = jnp.tanh(C0 * h * (1.0 + C1 * sq))
            half = 0.5 * (1.0 + th)
            act = (h * half).astype(jnp.bfloat16)
            slope = half + 0.5 * h * (1.0 - th * th) * (C0 * (1.0 + 3.0 * C1 * sq))
            own = pl.ds(k * bo, bo)
            act_ref[own, :] = act
            slope_ref[own, :] = slope.astype(jnp.bfloat16)
            v = dot_nn(w_out_ref[k], act)
            y_ref[rows, :] = (x_ref[rows, :].astype(jnp.float32) + v).astype(jnp.bfloat16)


def backward_kernel(
    x_ref, g_ref, w_in_ref, w_out_ref, gain_ref, act_ref, slope_ref,
    dx_ref, d_in_ref, d_out_ref, hid_ref, q_ref, r_ref, s_ref,
):
    step = pl.program_id(0)
    steps = pl.num_programs(0) // 2
    group, bi, bo = w_out_ref.shape
    nb = group * steps

    @pl.when(step == 0)
    def _():
        r_ref[...] = jnp.broadcast_to(inverse_rms(x_ref, bi), r_ref.shape)
        s_ref[...] = jnp.zeros_like(s_ref)

    @pl.when(step < steps)
    def _():
        for k in range(group):
            b = step * group + k
            g = g_ref[pl.ds(pl.multiple_of(b * bi, bi), bi), :]
            own = pl.ds(k * bo, bo)
            d_act = dot_tn(w_out_ref[k], g)
            hid_ref[pl.ds(pl.multiple_of(b * bo, bo), bo), :] = d_act * slope_ref[own, :].astype(
                jnp.float32
            )
            d_out_ref[k] = dot_nt(g, act_ref[own, :]).astype(jnp.bfloat16)

    @pl.when(step >= steps)
    def _():
        r = r_ref[0:1, :]
        for k in range(group):
            b = (step - steps) * group + k
            rows = pl.ds(pl.multiple_of(b * bi, bi), bi)
            d_hid = hid_ref[pl.ds(b, bo, stride=nb), :].astype(jnp.bfloat16)
            d_norm = dot_nn(w_in_ref[k, :bi, :], d_hid)
            x = x_ref[rows, :].astype(jnp.float32)
            gain = gain_ref[rows, :].astype(jnp.float32)
            unit = x * r
            normed = (unit * gain).astype(jnp.bfloat16)
            d_in_ref[k, :bi, :] = dot_nt(normed, d_hid).astype(jnp.bfloat16)
            extra = d_in_ref.shape[1] - bi
            ones = jnp.ones((extra, x.shape[1]), jnp.bfloat16)
            d_gain = dot_nt(ones, (d_norm * unit).astype(jnp.bfloat16))
            d_in_ref[k, bi:, :] = jnp.concatenate(
                [d_gain, jnp.zeros((extra, bo - bi), jnp.float32)], axis=1
            ).astype(jnp.bfloat16)
            q = d_norm * gain
            q_ref[rows, :] = q
            s_ref[...] += jnp.sum((q * x).reshape(bi // 8, 8, q.shape[1]), axis=0)

    @pl.when(step == 2 * steps - 1)
    def _():
        width = x_ref.shape[0]
        r = r_ref[0:1, :]
        s = jnp.sum(s_ref[...], axis=0, keepdims=True) * (r * r * r) / width

        def finish(i, carry):
            rows = pl.ds(pl.multiple_of(i * bi, bi), bi)
            x = x_ref[rows, :].astype(jnp.float32)
            g = g_ref[rows, :].astype(jnp.float32)
            dx_ref[rows, :] = (g + (q_ref[rows, :] * r - x * s)).astype(jnp.bfloat16)
            return carry

        lax.fori_loop(0, width // bi, finish, 0, unroll=4)


MESH = pl.DeviceIdType.MESH


def grid_of(dp):
    x = 1
    while 2 * (2 * x) * (2 * x) <= dp and dp % (2 * x) == 0:
        x = 2 * x
    return dp // x, x


class Place:
    def __init__(self, zs, xs):
        self.zs, self.xs = zs, xs
        self.segment = lax.axis_index("segment")
        self.me = lax.axis_index("dp")
        self.z, self.x = self.me // xs, self.me % xs

    def at(self, z, x):
        return (self.segment, z * self.xs + x)

    def beside(self, j):
        return lax.rem(self.x + j, self.xs)

    def enter(self, turns=False):
        barrier = pltpu.get_barrier_semaphore()

        def greet(z, x):
            pl.semaphore_signal(barrier, inc=1, device_id=self.at(z, x), device_id_type=MESH)

        for j in range(1, self.xs):
            greet(self.z, self.beside(j))

        @pl.when(self.z > 0)
        def _():
            greet(self.z - 1, self.x)

        @pl.when(self.z < self.zs - 1)
        def _():
            greet(self.z + 1, self.x)

        count = self.xs - 1 + jnp.where(self.z > 0, 1, 0) + jnp.where(self.z < self.zs - 1, 1, 0)
        if turns:
            odd = self.segment % 2 == 1

            @pl.when(odd)
            def _():
                pl.semaphore_signal(
                    barrier, inc=1, device_id=(self.segment - 1, self.me), device_id_type=MESH
                )

            leads = jnp.logical_not(odd) & (self.segment + 1 < lax.axis_size("segment"))
            count = count + jnp.where(leads, 1, 0)
        pl.semaphore_wait(barrier, count)

    def copy(self, src, dst, send, recv, z, x):
        return pltpu.make_async_remote_copy(
            src_ref=src, dst_ref=dst, send_sem=send, recv_sem=recv,
            device_id=self.at(z, x), device_id_type=MESH,
        )


def gather_kernel(
    zs, xs, a_ref, b_ref, ga_ref, gb_ref,
    turn_sem, own_sem, ax_send, ax_recv, bx_send, bx_recv, az_send, az_recv, bz_send, bz_recv,
):
    place = Place(zs, xs)
    z, x = place.z, place.x
    slots = a_ref.shape[0]
    place.enter(turns=True)
    turn = place.segment % 2

    @pl.when(turn == 1)
    def _():
        pl.semaphore_wait(turn_sem, 1)

    def own(l, which):
        src, dst = (a_ref, ga_ref) if which == 0 else (b_ref, gb_ref)
        return pltpu.make_async_copy(src.at[l], dst.at[l, z, x], own_sem.at[l, which])

    def a_beside(l, j, from_x):
        return place.copy(
            a_ref.at[l], ga_ref.at[l, z, from_x], ax_send.at[l, j], ax_recv.at[l, j],
            z, place.beside(j),
        )

    def b_beside(l, row, j, from_x):
        return place.copy(
            gb_ref.at[l, row, from_x], gb_ref.at[l, row, from_x],
            bx_send.at[l, row, j], bx_recv.at[l, row, j], z, place.beside(j),
        )

    def line(which, l, way, step, row, to_z):
        if which == 0:
            ref, send, recv = ga_ref.at[l, row], az_send, az_recv
        else:
            ref, send, recv = gb_ref.at[l, row, x], bz_send, bz_recv
        return place.copy(ref, ref, send.at[l, way, step], recv.at[l, way, step], to_z, x)

    def sends(which, l, step, act):
        @pl.when((z - step >= 0) & (z + 1 < zs))
        def _():
            act(line(which, l, 0, step, z - step, z + 1))

        @pl.when((z + step < zs) & (z - 1 >= 0))
        def _():
            act(line(which, l, 1, step, z + step, z - 1))

    def receives(which, l, step, then):
        @pl.when(z - 1 - step >= 0)
        def _():
            line(which, l, 0, step, z - 1 - step, z).wait_recv()
            then(z - 1 - step)

        @pl.when(z + 1 + step < zs)
        def _():
            line(which, l, 1, step, z + 1 + step, z).wait_recv()
            then(z + 1 + step)

    def begin(c):
        c.start()

    def done(c):
        c.wait_send()

    def spread(l, row):
        for j in range(1, xs):
            b_beside(l, row, j, x).start()

    for l in range(slots):
        own(l, 0).start()
        own(l, 1).start()
        for j in range(1, xs):
            a_beside(l, j, x).start()
    for l in range(slots):
        own(l, 1).wait()
        sends(1, l, 0, begin)
        spread(l, z)
    for l in range(slots):
        own(l, 0).wait()
        for j in range(1, xs):
            a_beside(l, j, lax.rem(x + xs - j, xs)).wait_recv()
        sends(0, l, 0, begin)
    for step in range(zs - 1):
        for l in range(slots):
            for which in (1, 0):
                receives(which, l, step, partial(spread, l) if which == 1 else lambda row: None)
                if step < zs - 2:
                    sends(which, l, step + 1, begin)
    for l in range(slots):
        for j in range(1, xs):
            a_beside(l, j, x).wait_send()
            for row in range(zs):
                b_beside(l, row, j, lax.rem(x + xs - j, xs)).wait_recv()
                b_beside(l, row, j, x).wait_send()
        for which in (0, 1):
            for step in range(zs - 1):
                sends(which, l, step, done)

    @pl.when((turn == 0) & (place.segment + 1 < lax.axis_size("segment")))
    def _():
        pl.semaphore_signal(
            turn_sem, inc=1, device_id=(place.segment + 1, place.me), device_id_type=MESH
        )


def gather_weights(a, b, dp):
    zs, xs = grid_of(dp)
    slots = a.shape[0]
    dma = pltpu.SemaphoreType.DMA
    ga, gb = pl.pallas_call(
        partial(gather_kernel, zs, xs),
        out_shape=tuple(
            jax.ShapeDtypeStruct((slots, zs, xs) + w.shape[1:], w.dtype) for w in (a, b)
        ),
        in_specs=[pl.BlockSpec(memory_space=pl.ANY)] * 2,
        out_specs=(pl.BlockSpec(memory_space=pl.ANY),) * 2,
        scratch_shapes=[pltpu.SemaphoreType.REGULAR, dma((slots, 2)), dma((slots, xs)), dma((slots, xs))]
        + [dma((slots, zs, xs))] * 2
        + [dma((slots, 2, zs))] * 4,
        compiler_params=pltpu.CompilerParams(
            collective_id=0, has_side_effects=True, vmem_limit_bytes=VMEM_BYTES
        ),
        name="gather_weights",
    )(a, b)
    return tuple(g.reshape((slots, -1) + g.shape[4:]) for g in (ga, gb))


def scatter_kernel(
    zs, xs, slots, *refs
):
    a_refs, b_refs = refs[:slots], refs[slots : 2 * slots]
    (
        oa_ref, ob_ref, a_line, b_line, a_sum, a_side, b_col, b_side,
        ax_send, ax_recv, bx_send, bx_recv, az_send, az_recv, bz_send, bz_recv,
    ) = refs[2 * slots :]
    place = Place(zs, xs)
    z, x = place.z, place.x
    n = a_refs[0].shape[2]
    f32, bf16 = jnp.float32, jnp.bfloat16
    place.enter()

    def each(count, body):
        def step(i, carry):
            body(i)
            return carry

        lax.fori_loop(0, count, step, 0)

    def b_beside(l, j):
        return place.copy(
            b_refs[l].at[:, place.beside(j)], b_side.at[l, j], bx_send.at[l, j], bx_recv.at[l, j],
            z, place.beside(j),
        )

    def a_beside(l, j):
        return place.copy(
            a_sum.at[l, place.beside(j)], a_side.at[l, j], ax_send.at[l, j], ax_recv.at[l, j],
            z, place.beside(j),
        )

    def mine(which, l, row):
        return a_refs[l].at[row] if which == 0 else b_col.at[l, row]

    def line(which, l, way, step, src, to_z):
        buf, send, recv = (
            (a_line, az_send, az_recv) if which == 0 else (b_line, bz_send, bz_recv)
        )
        return place.copy(
            src, buf.at[l, way, step], send.at[l, way, step], recv.at[l, way, step], to_z, x
        )

    def row_of(way, step):
        return zs - 1 - step if way == 0 else step

    def advance(which, l, way, step):
        buf = (a_line if which == 0 else b_line).at[l, way, step]
        row = row_of(way, step)
        own = mine(which, l, row)
        to_z = z + 1 if way == 0 else z - 1
        first = z == 0 if way == 0 else z == zs - 1
        beyond = z < row if way == 0 else z > row
        ahead = z <= row if way == 0 else z >= row

        @pl.when(jnp.logical_not(first) & ahead)
        def _():
            line(which, l, way, step, buf, z).wait_recv()

        @pl.when(jnp.logical_not(first) & beyond)
        def _():
            def add(i):
                at = (i // n, i % n) if which == 0 else (i,)
                buf[at] = (buf[at].astype(f32) + own[at].astype(f32)).astype(bf16)

            each(xs * n if which == 0 else n, add)
            line(which, l, way, step, buf, to_z).start()

        @pl.when(first & beyond)
        def _():
            line(which, l, way, step, own, to_z).start()

    def finish_sends(which, l, way, step):
        row = row_of(way, step)

        @pl.when(z < row if way == 0 else z > row)
        def _():
            buf = (a_line if which == 0 else b_line).at[l, way, step]
            line(which, l, way, step, buf, z + 1 if way == 0 else z - 1).wait_send()

    for l in reversed(range(slots)):
        for j in range(1, xs):
            b_beside(l, j).start()
    def move(which, l, tick):
        for way in (0, 1):
            step = tick - (z if way == 0 else zs - 1 - z)

            @pl.when((step >= 0) & (step < zs - 1))
            def _(way=way, step=step):
                advance(which, l, way, step)

    for l in reversed(range(slots)):
        move(0, l, 0)
    for l in reversed(range(slots)):
        for j in range(1, xs):
            b_beside(l, j).wait_recv()

        def column(i, l=l):
            row, k = i // n, i % n
            value = b_refs[l][row, x, k].astype(f32)
            for j in range(1, xs):
                value += b_side[l, j, row, k].astype(f32)
            b_col[l, row, k] = value.astype(bf16)

        each(zs * n, column)
        move(1, l, 0)

    def tick(t, carry):
        for l in reversed(range(slots)):
            for which in (0, 1):
                move(which, l, t)
        return carry

    lax.fori_loop(1, 2 * zs - 2, tick, 0)

    for l in reversed(range(slots)):
        right, left = jnp.clip(zs - 1 - z, 0, zs - 2), jnp.clip(z, 0, zs - 2)
        has_right, has_left = z > 0, z < zs - 1

        def start_sum(i, l=l):
            p, k = i // n, i % n
            a_sum[l, p, k] = a_refs[l][z, p, k]

        def add_sum(way, at, i, l=l):
            p, k = i // n, i % n
            a_sum[l, p, k] = (
                a_sum[l, p, k].astype(f32) + a_line[l, way, at, p, k].astype(f32)
            ).astype(bf16)

        each(xs * n, start_sum)
        pl.when(has_right)(lambda: each(xs * n, partial(add_sum, 0, right)))
        pl.when(has_left)(lambda: each(xs * n, partial(add_sum, 1, left)))
        for j in range(1, xs):
            a_beside(l, j).start()

        def start_out(i, l=l):
            ob_ref[l, i] = b_col[l, z, i].astype(f32)

        def add_out(way, at, i, l=l):
            ob_ref[l, i] += b_line[l, way, at, i].astype(f32)

        each(n, start_out)
        pl.when(has_right)(lambda: each(n, partial(add_out, 0, right)))
        pl.when(has_left)(lambda: each(n, partial(add_out, 1, left)))
    for l in reversed(range(slots)):
        for j in range(1, xs):
            a_beside(l, j).wait_recv()

        def out(i, l=l):
            value = a_sum[l, x, i].astype(f32)
            for j in range(1, xs):
                value += a_side[l, j, i].astype(f32)
            oa_ref[l, i] = value

        each(n, out)
    for l in range(slots):
        for j in range(1, xs):
            a_beside(l, j).wait_send()
            b_beside(l, j).wait_send()
        for which in (0, 1):
            for way in (0, 1):
                for step in range(zs - 1):
                    finish_sends(which, l, way, step)


def scatter_grads(a, b, dp):
    zs, xs = grid_of(dp)
    slots, nb = len(a), a[0].shape[0]
    n = nb // dp
    a, b = ([g.reshape((zs, xs, n) + g.shape[1:]) for g in own] for own in (a, b))
    ta, tb = a[0].shape[3:], b[0].shape[3:]
    dma = pltpu.SemaphoreType.DMA
    bf16 = jnp.bfloat16
    vmem = pl.BlockSpec(memory_space=pltpu.VMEM)
    return pl.pallas_call(
        partial(scatter_kernel, zs, xs, slots),
        out_shape=tuple(
            jax.ShapeDtypeStruct((slots, n) + t, jnp.float32) for t in (ta, tb)
        ),
        in_specs=[vmem] * (2 * slots),
        out_specs=(vmem, vmem),
        scratch_shapes=[
            pltpu.VMEM((slots, 2, zs - 1, xs, n) + ta, bf16),
            pltpu.VMEM((slots, 2, zs - 1, n) + tb, bf16),
            pltpu.VMEM((slots, xs, n) + ta, bf16),
            pltpu.VMEM((slots, xs, n) + ta, bf16),
            pltpu.VMEM((slots, zs, n) + tb, bf16),
            pltpu.VMEM((slots, xs, zs, n) + tb, bf16),
        ]
        + [dma((slots, xs))] * 4
        + [dma((slots, 2, zs))] * 4,
        compiler_params=pltpu.CompilerParams(
            collective_id=1, has_side_effects=True, vmem_limit_bytes=VMEM_BYTES
        ),
        name="scatter_grads",
    )(*a, *b)


def whole(shape):
    return pl.BlockSpec(shape, lambda i: (0,) * len(shape))


def forward_layer(slot, x, w_in, w_out, gain):
    width, tokens = x.shape
    nb, bi, bo = w_out.shape[1:]
    wide = w_in.shape[2]
    group = min(GROUP, nb)
    steps = nb // group
    second2 = lambda i: (jnp.maximum(i - steps, 0), 0)
    slot_first = lambda i: (slot, jnp.minimum(i, steps - 1), 0, 0)
    slot_second = lambda i: (slot, jnp.maximum(i - steps, 0), 0, 0)
    return pl.pallas_call(
        forward_kernel,
        grid=(2 * steps,),
        out_shape=(
            jax.ShapeDtypeStruct((width, tokens), jnp.bfloat16),
            jax.ShapeDtypeStruct((nb * bo, tokens), jnp.bfloat16),
            jax.ShapeDtypeStruct((nb * bo, tokens), jnp.bfloat16),
        ),
        in_specs=[
            whole((width, tokens)),
            pl.BlockSpec((None, group, wide, bo), slot_first),
            pl.BlockSpec((None, group, bi, bo), slot_second),
            whole((width, tokens)),
        ],
        out_specs=(
            whole((width, tokens)),
            pl.BlockSpec((group * bo, tokens), second2),
            pl.BlockSpec((group * bo, tokens), second2),
        ),
        scratch_shapes=[
            pltpu.VMEM((nb * bo, tokens), jnp.float32),
            pltpu.VMEM((8, tokens), jnp.float32),
        ],
        compiler_params=pltpu.CompilerParams(vmem_limit_bytes=VMEM_BYTES),
        name="layer_forward",
    )(x, w_in, w_out, gain)


def backward_layer(slot, x, g, w_in, w_out, gain, act, slope):
    width, tokens = x.shape
    nb, bi, bo = w_out.shape[1:]
    wide = w_in.shape[2]
    group = min(GROUP, nb)
    steps = nb // group
    first = lambda i: (jnp.minimum(i, steps - 1), 0, 0)
    first2 = lambda i: (jnp.minimum(i, steps - 1), 0)
    second = lambda i: (jnp.maximum(i - steps, 0), 0, 0)
    slot_first = lambda i: (slot, jnp.minimum(i, steps - 1), 0, 0)
    slot_second = lambda i: (slot, jnp.maximum(i - steps, 0), 0, 0)
    return pl.pallas_call(
        backward_kernel,
        grid=(2 * steps,),
        out_shape=(
            jax.ShapeDtypeStruct((width, tokens), jnp.bfloat16),
            jax.ShapeDtypeStruct((nb, wide, bo), jnp.bfloat16),
            jax.ShapeDtypeStruct((nb, bi, bo), jnp.bfloat16),
        ),
        in_specs=[
            whole((width, tokens)),
            whole((width, tokens)),
            pl.BlockSpec((None, group, wide, bo), slot_second),
            pl.BlockSpec((None, group, bi, bo), slot_first),
            whole((width, tokens)),
            pl.BlockSpec((group * bo, tokens), first2),
            pl.BlockSpec((group * bo, tokens), first2),
        ],
        out_specs=(
            whole((width, tokens)),
            pl.BlockSpec((group, wide, bo), second),
            pl.BlockSpec((group, bi, bo), first),
        ),
        scratch_shapes=[
            pltpu.VMEM((nb * bo, tokens), jnp.float32),
            pltpu.VMEM((width, tokens), jnp.float32),
            pltpu.VMEM((8, tokens), jnp.float32),
            pltpu.VMEM((8, tokens), jnp.float32),
        ],
        compiler_params=pltpu.CompilerParams(vmem_limit_bytes=VMEM_BYTES),
        name="layer_backward",
    )(x, g, w_in, w_out, gain, act, slope)


def to_columns(a):
    micro, rows, width = a.shape
    return a.reshape(micro * rows, width).T


def per_device(inputs, cotangent, w_in, w_out, gains, counts):
    segment_count = lax.axis_size("segment")
    my_segment = lax.axis_index("segment")
    slot_count = w_in.shape[1]
    micro, rows, width = inputs.shape
    tokens = micro * rows
    count_here = jnp.sum(jnp.where(jnp.arange(segment_count) == my_segment, counts, 0))
    dp = lax.axis_size("dp")
    own_nb, bi, bo = w_in.shape[2:]
    nb = own_nb * dp
    extra = 16
    gain_rows = jnp.pad(
        gains.reshape(slot_count, own_nb, 1, bi), ((0, 0), (0, 0), (0, extra - 1), (0, bo - bi))
    )
    full_in, full_out = gather_weights(
        jnp.concatenate([w_in[0], gain_rows], axis=2), w_out[0], dp
    )
    gain = [
        jnp.broadcast_to(full_in[l, :, bi, :bi].reshape(width, 1), (width, tokens))
        for l in range(slot_count)
    ]
    first_x = to_columns(inputs)
    last_g = to_columns(cotangent)

    def run_forward(operands):
        x, saved = operands
        kept = []
        for l in range(slot_count):
            def live(x, l=l):
                return forward_layer(l, x, full_in, full_out, gain[l])

            if l == 0:
                y, act, slope = live(x)
            else:
                y, act, slope = lax.cond(
                    l < count_here, live, lambda x, l=l: (x, saved[l][1], saved[l][2]), x
                )
            kept.append((x, act, slope))
            x = y
        return x, tuple(kept)

    def keep(operands):
        return operands

    hid = jnp.zeros((nb * bo, tokens), jnp.bfloat16)
    saved = tuple((first_x, hid, hid) for l in range(slot_count))
    x = first_x
    result = x
    for k in range(segment_count):
        x, saved = lax.cond(my_segment == k, run_forward, keep, (x, saved))
        result = jnp.where(my_segment == k, x, result)
        if k < segment_count - 1:
            x = lax.ppermute(x, "segment", [(k, k + 1)])

    def run_backward(operands):
        g, grads = operands
        out = [None] * slot_count
        for l in reversed(range(slot_count)):
            x, act, slope = saved[l]

            def live(g, l=l, x=x, act=act, slope=slope):
                return backward_layer(l, x, g, full_in, full_out, gain[l], act, slope)

            if l == 0:
                g, *out[l] = live(g)
            else:
                g, *out[l] = lax.cond(l < count_here, live, lambda g, l=l: (g, *grads[l]), g)
        return g, tuple(tuple(o) for o in out)

    zero_in = jnp.zeros((nb, bi + extra, bo), jnp.bfloat16)
    zero_out = jnp.zeros((nb, bi, bo), jnp.bfloat16)
    grads = tuple((zero_in, zero_out) for l in range(slot_count))
    g = last_g
    down = g
    for k in reversed(range(segment_count)):
        g, grads = lax.cond(my_segment == k, run_backward, keep, (g, grads))
        down = jnp.where(my_segment == k, g, down)
        if k > 0:
            g = lax.ppermute(g, "segment", [(k, k - 1)])

    sum_in, sum_out = scatter_grads(
        [grads[l][0] for l in range(slot_count)],
        [grads[l][1] for l in range(slot_count)],
        dp,
    )
    grad_in = sum_in[None, :, :, :bi, :]
    grad_out = sum_out[None]
    grad_gain = sum_in[:, :, bi, :bi].reshape(1, slot_count, own_nb * bi)
    outputs = result.T.reshape(1, micro, rows, width)
    grads_kept = down.T.reshape(1, micro, rows, width)
    return outputs, grads_kept, grad_in, grad_out, grad_gain


def solution(mesh):
    in_specs = (
        P(None, "dp", None),
        P(None, "dp", None),
        P("segment", None, "dp", None, None),
        P("segment", None, "dp", None, None),
        P("segment", None, "dp"),
        P(),
    )
    out_specs = (
        P("segment", None, "dp", None),
        P("segment", None, "dp", None),
        P("segment", None, "dp", None, None),
        P("segment", None, "dp", None, None),
        P("segment", None, "dp"),
    )
    return jax.shard_map(
        per_device, mesh=mesh, in_specs=in_specs, out_specs=out_specs, check_vma=False
    )
```

```python
from functools import partial

import jax
import jax.numpy as jnp
from jax import lax
from jax.experimental import pallas as pl
from jax.experimental.pallas import tpu as pltpu
from jax.sharding import PartitionSpec as P

EPS = 1e-05
GROUP = 16
VMEM_BYTES = 48 * 1024 * 1024
C0 = 0.7978845608028654
C1 = 0.044715


def dot_tn(a, b):
    return lax.dot_general(a, b, (((0,), (0,)), ((), ())), preferred_element_type=jnp.float32)


def dot_nt(a, b):
    return lax.dot_general(a, b, (((1,), (1,)), ((), ())), preferred_element_type=jnp.float32)


def dot_nn(a, b):
    return lax.dot_general(a, b, (((1,), (0,)), ((), ())), preferred_element_type=jnp.float32)


def inverse_rms(x_ref, chunk):
    width, tokens = x_ref.shape

    def add(i, total):
        x = x_ref[pl.ds(pl.multiple_of(i * chunk, chunk), chunk), :].astype(jnp.float32)
        return total + jnp.sum((x * x).reshape(chunk // 8, 8, tokens), axis=0)

    total = lax.fori_loop(0, width // chunk, add, jnp.zeros((8, tokens), jnp.float32), unroll=4)
    mean = jnp.sum(total, axis=0, keepdims=True) / width
    return lax.rsqrt(mean + EPS)


def forward_kernel(x_ref, w_in_ref, w_out_ref, gain_ref, y_ref, act_ref, slope_ref, hid_ref, r_ref):
    step = pl.program_id(0)
    steps = pl.num_programs(0) // 2
    group, bi, bo = w_out_ref.shape
    nb = group * steps

    @pl.when(step == 0)
    def _():
        r_ref[...] = jnp.broadcast_to(inverse_rms(x_ref, bi), r_ref.shape)

    @pl.when(step < steps)
    def _():
        r = r_ref[0:1, :]
        for k in range(group):
            b = step * group + k
            rows = pl.ds(pl.multiple_of(b * bi, bi), bi)
            x = x_ref[rows, :].astype(jnp.float32)
            normed = (x * r * gain_ref[rows, :].astype(jnp.float32)).astype(jnp.bfloat16)
            hid_ref[pl.ds(b, bo, stride=nb), :] = dot_tn(w_in_ref[k, :bi, :], normed)

    @pl.when(step >= steps)
    def _():
        for k in range(group):
            b = (step - steps) * group + k
            rows = pl.ds(pl.multiple_of(b * bi, bi), bi)
            h = hid_ref[pl.ds(pl.multiple_of(b * bo, bo), bo), :]
            sq = h * h
            th = jnp.tanh(C0 * h * (1.0 + C1 * sq))
            half = 0.5 * (1.0 + th)
            act = (h * half).astype(jnp.bfloat16)
            slope = half + 0.5 * h * (1.0 - th * th) * (C0 * (1.0 + 3.0 * C1 * sq))
            own = pl.ds(k * bo, bo)
            act_ref[own, :] = act
            slope_ref[own, :] = slope.astype(jnp.bfloat16)
            v = dot_nn(w_out_ref[k], act)
            y_ref[rows, :] = (x_ref[rows, :].astype(jnp.float32) + v).astype(jnp.bfloat16)


def backward_kernel(
    x_ref, g_ref, w_in_ref, w_out_ref, gain_ref, act_ref, slope_ref,
    dx_ref, d_in_ref, d_out_ref, hid_ref, q_ref, r_ref, s_ref,
):
    step = pl.program_id(0)
    steps = pl.num_programs(0) // 2
    group, bi, bo = w_out_ref.shape
    nb = group * steps

    @pl.when(step == 0)
    def _():
        r_ref[...] = jnp.broadcast_to(inverse_rms(x_ref, bi), r_ref.shape)
        s_ref[...] = jnp.zeros_like(s_ref)

    @pl.when(step < steps)
    def _():
        for k in range(group):
            b = step * group + k
            g = g_ref[pl.ds(pl.multiple_of(b * bi, bi), bi), :]
            own = pl.ds(k * bo, bo)
            d_act = dot_tn(w_out_ref[k], g)
            hid_ref[pl.ds(pl.multiple_of(b * bo, bo), bo), :] = d_act * slope_ref[own, :].astype(
                jnp.float32
            )
            d_out_ref[k] = dot_nt(g, act_ref[own, :]).astype(jnp.bfloat16)

    @pl.when(step >= steps)
    def _():
        r = r_ref[0:1, :]
        for k in range(group):
            b = (step - steps) * group + k
            rows = pl.ds(pl.multiple_of(b * bi, bi), bi)
            d_hid = hid_ref[pl.ds(b, bo, stride=nb), :].astype(jnp.bfloat16)
            d_norm = dot_nn(w_in_ref[k, :bi, :], d_hid)
            x = x_ref[rows, :].astype(jnp.float32)
            gain = gain_ref[rows, :].astype(jnp.float32)
            unit = x * r
            normed = (unit * gain).astype(jnp.bfloat16)
            d_in_ref[k, :bi, :] = dot_nt(normed, d_hid).astype(jnp.bfloat16)
            extra = d_in_ref.shape[1] - bi
            ones = jnp.ones((extra, x.shape[1]), jnp.bfloat16)
            d_gain = dot_nt(ones, (d_norm * unit).astype(jnp.bfloat16))
            d_in_ref[k, bi:, :] = jnp.concatenate(
                [d_gain, jnp.zeros((extra, bo - bi), jnp.float32)], axis=1
            ).astype(jnp.bfloat16)
            q = d_norm * gain
            q_ref[rows, :] = q
            s_ref[...] += jnp.sum((q * x).reshape(bi // 8, 8, q.shape[1]), axis=0)

    @pl.when(step == 2 * steps - 1)
    def _():
        width = x_ref.shape[0]
        r = r_ref[0:1, :]
        s = jnp.sum(s_ref[...], axis=0, keepdims=True) * (r * r * r) / width

        def finish(i, carry):
            rows = pl.ds(pl.multiple_of(i * bi, bi), bi)
            x = x_ref[rows, :].astype(jnp.float32)
            g = g_ref[rows, :].astype(jnp.float32)
            dx_ref[rows, :] = (g + (q_ref[rows, :] * r - x * s)).astype(jnp.bfloat16)
            return carry

        lax.fori_loop(0, width // bi, finish, 0, unroll=4)


MESH = pl.DeviceIdType.MESH


def grid_of(dp):
    x = 1
    while 2 * (2 * x) * (2 * x) <= dp and dp % (2 * x) == 0:
        x = 2 * x
    return dp // x, x


class Place:
    def __init__(self, zs, xs):
        self.zs, self.xs = zs, xs
        self.segment = lax.axis_index("segment")
        self.me = lax.axis_index("dp")
        self.z, self.x = self.me // xs, self.me % xs

    def at(self, z, x):
        return (self.segment, z * self.xs + x)

    def beside(self, j):
        return lax.rem(self.x + j, self.xs)

    def enter(self, turns=False):
        barrier = pltpu.get_barrier_semaphore()

        def greet(z, x):
            pl.semaphore_signal(barrier, inc=1, device_id=self.at(z, x), device_id_type=MESH)

        for j in range(1, self.xs):
            greet(self.z, self.beside(j))

        @pl.when(self.z > 0)
        def _():
            greet(self.z - 1, self.x)

        @pl.when(self.z < self.zs - 1)
        def _():
            greet(self.z + 1, self.x)

        count = self.xs - 1 + jnp.where(self.z > 0, 1, 0) + jnp.where(self.z < self.zs - 1, 1, 0)
        if turns:
            odd = self.segment % 2 == 1

            @pl.when(odd)
            def _():
                pl.semaphore_signal(
                    barrier, inc=1, device_id=(self.segment - 1, self.me), device_id_type=MESH
                )

            leads = jnp.logical_not(odd) & (self.segment + 1 < lax.axis_size("segment"))
            count = count + jnp.where(leads, 1, 0)
        pl.semaphore_wait(barrier, count)

    def copy(self, src, dst, send, recv, z, x):
        return pltpu.make_async_remote_copy(
            src_ref=src, dst_ref=dst, send_sem=send, recv_sem=recv,
            device_id=self.at(z, x), device_id_type=MESH,
        )


def gather_kernel(
    zs, xs, a_ref, b_ref, ga_ref, gb_ref,
    turn_sem, own_sem, ax_send, ax_recv, bx_send, bx_recv, az_send, az_recv, bz_send, bz_recv,
):
    place = Place(zs, xs)
    z, x = place.z, place.x
    slots = a_ref.shape[0]
    place.enter(turns=True)
    turn = place.segment % 2

    @pl.when(turn == 1)
    def _():
        pl.semaphore_wait(turn_sem, 1)

    def own(l, which):
        src, dst = (a_ref, ga_ref) if which == 0 else (b_ref, gb_ref)
        return pltpu.make_async_copy(src.at[l], dst.at[l, z, x], own_sem.at[l, which])

    def a_beside(l, j, from_x):
        return place.copy(
            a_ref.at[l], ga_ref.at[l, z, from_x], ax_send.at[l, j], ax_recv.at[l, j],
            z, place.beside(j),
        )

    def b_beside(l, row, j, from_x):
        return place.copy(
            gb_ref.at[l, row, from_x], gb_ref.at[l, row, from_x],
            bx_send.at[l, row, j], bx_recv.at[l, row, j], z, place.beside(j),
        )

    def line(which, l, way, step, row, to_z):
        if which == 0:
            ref, send, recv = ga_ref.at[l, row], az_send, az_recv
        else:
            ref, send, recv = gb_ref.at[l, row, x], bz_send, bz_recv
        return place.copy(ref, ref, send.at[l, way, step], recv.at[l, way, step], to_z, x)

    def sends(which, l, step, act):
        @pl.when((z - step >= 0) & (z + 1 < zs))
        def _():
            act(line(which, l, 0, step, z - step, z + 1))

        @pl.when((z + step < zs) & (z - 1 >= 0))
        def _():
            act(line(which, l, 1, step, z + step, z - 1))

    def receives(which, l, step, then):
        @pl.when(z - 1 - step >= 0)
        def _():
            line(which, l, 0, step, z - 1 - step, z).wait_recv()
            then(z - 1 - step)

        @pl.when(z + 1 + step < zs)
        def _():
            line(which, l, 1, step, z + 1 + step, z).wait_recv()
            then(z + 1 + step)

    def begin(c):
        c.start()

    def done(c):
        c.wait_send()

    def spread(l, row):
        for j in range(1, xs):
            b_beside(l, row, j, x).start()

    for l in range(slots):
        own(l, 0).start()
        own(l, 1).start()
        for j in range(1, xs):
            a_beside(l, j, x).start()
    for l in range(slots):
        own(l, 1).wait()
        sends(1, l, 0, begin)
        spread(l, z)
    for l in range(slots):
        own(l, 0).wait()
        for j in range(1, xs):
            a_beside(l, j, lax.rem(x + xs - j, xs)).wait_recv()
        sends(0, l, 0, begin)
    for step in range(zs - 1):
        for l in range(slots):
            for which in (1, 0):
                receives(which, l, step, partial(spread, l) if which == 1 else lambda row: None)
                if step < zs - 2:
                    sends(which, l, step + 1, begin)
    for l in range(slots):
        for j in range(1, xs):
            a_beside(l, j, x).wait_send()
            for row in range(zs):
                b_beside(l, row, j, lax.rem(x + xs - j, xs)).wait_recv()
                b_beside(l, row, j, x).wait_send()
        for which in (0, 1):
            for step in range(zs - 1):
                sends(which, l, step, done)

    @pl.when((turn == 0) & (place.segment + 1 < lax.axis_size("segment")))
    def _():
        pl.semaphore_signal(
            turn_sem, inc=1, device_id=(place.segment + 1, place.me), device_id_type=MESH
        )


def gather_weights(a, b, dp):
    zs, xs = grid_of(dp)
    slots = a.shape[0]
    dma = pltpu.SemaphoreType.DMA
    ga, gb = pl.pallas_call(
        partial(gather_kernel, zs, xs),
        out_shape=tuple(
            jax.ShapeDtypeStruct((slots, zs, xs) + w.shape[1:], w.dtype) for w in (a, b)
        ),
        in_specs=[pl.BlockSpec(memory_space=pl.ANY)] * 2,
        out_specs=(pl.BlockSpec(memory_space=pl.ANY),) * 2,
        scratch_shapes=[pltpu.SemaphoreType.REGULAR, dma((slots, 2)), dma((slots, xs)), dma((slots, xs))]
        + [dma((slots, zs, xs))] * 2
        + [dma((slots, 2, zs))] * 4,
        compiler_params=pltpu.CompilerParams(
            collective_id=0, has_side_effects=True, vmem_limit_bytes=VMEM_BYTES
        ),
        name="gather_weights",
    )(a, b)
    return tuple(g.reshape((slots, -1) + g.shape[4:]) for g in (ga, gb))


def scatter_kernel(
    zs, xs, slots, *refs
):
    a_refs, b_refs = refs[:slots], refs[slots : 2 * slots]
    (
        oa_ref, ob_ref, a_line, b_line, a_sum, a_side, b_col, b_side,
        ax_send, ax_recv, bx_send, bx_recv, az_send, az_recv, bz_send, bz_recv,
    ) = refs[2 * slots :]
    place = Place(zs, xs)
    z, x = place.z, place.x
    n = a_refs[0].shape[2]
    f32, bf16 = jnp.float32, jnp.bfloat16
    place.enter()

    def each(count, body):
        def step(i, carry):
            body(i)
            return carry

        lax.fori_loop(0, count, step, 0)

    def b_beside(l, j):
        return place.copy(
            b_refs[l].at[:, place.beside(j)], b_side.at[l, j], bx_send.at[l, j], bx_recv.at[l, j],
            z, place.beside(j),
        )

    def a_beside(l, j):
        return place.copy(
            a_sum.at[l, place.beside(j)], a_side.at[l, j], ax_send.at[l, j], ax_recv.at[l, j],
            z, place.beside(j),
        )

    def mine(which, l, row):
        return a_refs[l].at[row] if which == 0 else b_col.at[l, row]

    def line(which, l, way, step, src, to_z):
        buf, send, recv = (
            (a_line, az_send, az_recv) if which == 0 else (b_line, bz_send, bz_recv)
        )
        return place.copy(
            src, buf.at[l, way, step], send.at[l, way, step], recv.at[l, way, step], to_z, x
        )

    def row_of(way, step):
        return zs - 1 - step if way == 0 else step

    def advance(which, l, way, step):
        buf = (a_line if which == 0 else b_line).at[l, way, step]
        row = row_of(way, step)
        own = mine(which, l, row)
        to_z = z + 1 if way == 0 else z - 1
        first = z == 0 if way == 0 else z == zs - 1
        beyond = z < row if way == 0 else z > row
        ahead = z <= row if way == 0 else z >= row

        @pl.when(jnp.logical_not(first) & ahead)
        def _():
            line(which, l, way, step, buf, z).wait_recv()

        @pl.when(jnp.logical_not(first) & beyond)
        def _():
            def add(i):
                at = (i // n, i % n) if which == 0 else (i,)
                buf[at] = (buf[at].astype(f32) + own[at].astype(f32)).astype(bf16)

            each(xs * n if which == 0 else n, add)
            line(which, l, way, step, buf, to_z).start()

        @pl.when(first & beyond)
        def _():
            line(which, l, way, step, own, to_z).start()

    def finish_sends(which, l, way, step):
        row = row_of(way, step)

        @pl.when(z < row if way == 0 else z > row)
        def _():
            buf = (a_line if which == 0 else b_line).at[l, way, step]
            line(which, l, way, step, buf, z + 1 if way == 0 else z - 1).wait_send()

    for l in reversed(range(slots)):
        for j in range(1, xs):
            b_beside(l, j).start()
    def move(which, l, tick):
        for way in (0, 1):
            step = tick - (z if way == 0 else zs - 1 - z)

            @pl.when((step >= 0) & (step < zs - 1))
            def _(way=way, step=step):
                advance(which, l, way, step)

    for l in reversed(range(slots)):
        move(0, l, 0)
    for l in reversed(range(slots)):
        for j in range(1, xs):
            b_beside(l, j).wait_recv()

        def column(i, l=l):
            row, k = i // n, i % n
            value = b_refs[l][row, x, k].astype(f32)
            for j in range(1, xs):
                value += b_side[l, j, row, k].astype(f32)
            b_col[l, row, k] = value.astype(bf16)

        each(zs * n, column)
        move(1, l, 0)

    def tick(t, carry):
        for l in reversed(range(slots)):
            for which in (0, 1):
                move(which, l, t)
        return carry

    lax.fori_loop(1, 2 * zs - 2, tick, 0)

    for l in reversed(range(slots)):
        right, left = jnp.clip(zs - 1 - z, 0, zs - 2), jnp.clip(z, 0, zs - 2)
        has_right, has_left = z > 0, z < zs - 1

        def start_sum(i, l=l):
            p, k = i // n, i % n
            a_sum[l, p, k] = a_refs[l][z, p, k]

        def add_sum(way, at, i, l=l):
            p, k = i // n, i % n
            a_sum[l, p, k] = (
                a_sum[l, p, k].astype(f32) + a_line[l, way, at, p, k].astype(f32)
            ).astype(bf16)

        each(xs * n, start_sum)
        pl.when(has_right)(lambda: each(xs * n, partial(add_sum, 0, right)))
        pl.when(has_left)(lambda: each(xs * n, partial(add_sum, 1, left)))
        for j in range(1, xs):
            a_beside(l, j).start()

        def start_out(i, l=l):
            ob_ref[l, i] = b_col[l, z, i].astype(f32)

        def add_out(way, at, i, l=l):
            ob_ref[l, i] += b_line[l, way, at, i].astype(f32)

        each(n, start_out)
        pl.when(has_right)(lambda: each(n, partial(add_out, 0, right)))
        pl.when(has_left)(lambda: each(n, partial(add_out, 1, left)))
    for l in reversed(range(slots)):
        for j in range(1, xs):
            a_beside(l, j).wait_recv()

        def out(i, l=l):
            value = a_sum[l, x, i].astype(f32)
            for j in range(1, xs):
                value += a_side[l, j, i].astype(f32)
            oa_ref[l, i] = value

        each(n, out)
    for l in range(slots):
        for j in range(1, xs):
            a_beside(l, j).wait_send()
            b_beside(l, j).wait_send()
        for which in (0, 1):
            for way in (0, 1):
                for step in range(zs - 1):
                    finish_sends(which, l, way, step)


def scatter_grads(a, b, dp):
    zs, xs = grid_of(dp)
    slots, nb = len(a), a[0].shape[0]
    n = nb // dp
    a, b = ([g.reshape((zs, xs, n) + g.shape[1:]) for g in own] for own in (a, b))
    ta, tb = a[0].shape[3:], b[0].shape[3:]
    dma = pltpu.SemaphoreType.DMA
    bf16 = jnp.bfloat16
    vmem = pl.BlockSpec(memory_space=pltpu.VMEM)
    return pl.pallas_call(
        partial(scatter_kernel, zs, xs, slots),
        out_shape=tuple(
            jax.ShapeDtypeStruct((slots, n) + t, jnp.float32) for t in (ta, tb)
        ),
        in_specs=[vmem] * (2 * slots),
        out_specs=(vmem, vmem),
        scratch_shapes=[
            pltpu.VMEM((slots, 2, zs - 1, xs, n) + ta, bf16),
            pltpu.VMEM((slots, 2, zs - 1, n) + tb, bf16),
            pltpu.VMEM((slots, xs, n) + ta, bf16),
            pltpu.VMEM((slots, xs, n) + ta, bf16),
            pltpu.VMEM((slots, zs, n) + tb, bf16),
            pltpu.VMEM((slots, xs, zs, n) + tb, bf16),
        ]
        + [dma((slots, xs))] * 4
        + [dma((slots, 2, zs))] * 4,
        compiler_params=pltpu.CompilerParams(
            collective_id=1, has_side_effects=True, vmem_limit_bytes=VMEM_BYTES
        ),
        name="scatter_grads",
    )(*a, *b)


def whole(shape):
    return pl.BlockSpec(shape, lambda i: (0,) * len(shape))


def forward_layer(slot, x, w_in, w_out, gain):
    width, tokens = x.shape
    nb, bi, bo = w_out.shape[1:]
    wide = w_in.shape[2]
    group = min(GROUP, nb)
    steps = nb // group
    second2 = lambda i: (jnp.maximum(i - steps, 0), 0)
    slot_first = lambda i: (slot, jnp.minimum(i, steps - 1), 0, 0)
    slot_second = lambda i: (slot, jnp.maximum(i - steps, 0), 0, 0)
    return pl.pallas_call(
        forward_kernel,
        grid=(2 * steps,),
        out_shape=(
            jax.ShapeDtypeStruct((width, tokens), jnp.bfloat16),
            jax.ShapeDtypeStruct((nb * bo, tokens), jnp.bfloat16),
            jax.ShapeDtypeStruct((nb * bo, tokens), jnp.bfloat16),
        ),
        in_specs=[
            whole((width, tokens)),
            pl.BlockSpec((None, group, wide, bo), slot_first),
            pl.BlockSpec((None, group, bi, bo), slot_second),
            whole((width, tokens)),
        ],
        out_specs=(
            whole((width, tokens)),
            pl.BlockSpec((group * bo, tokens), second2),
            pl.BlockSpec((group * bo, tokens), second2),
        ),
        scratch_shapes=[
            pltpu.VMEM((nb * bo, tokens), jnp.float32),
            pltpu.VMEM((8, tokens), jnp.float32),
        ],
        compiler_params=pltpu.CompilerParams(vmem_limit_bytes=VMEM_BYTES),
        name="layer_forward",
    )(x, w_in, w_out, gain)


def backward_layer(slot, x, g, w_in, w_out, gain, act, slope):
    width, tokens = x.shape
    nb, bi, bo = w_out.shape[1:]
    wide = w_in.shape[2]
    group = min(GROUP, nb)
    steps = nb // group
    first = lambda i: (jnp.minimum(i, steps - 1), 0, 0)
    first2 = lambda i: (jnp.minimum(i, steps - 1), 0)
    second = lambda i: (jnp.maximum(i - steps, 0), 0, 0)
    slot_first = lambda i: (slot, jnp.minimum(i, steps - 1), 0, 0)
    slot_second = lambda i: (slot, jnp.maximum(i - steps, 0), 0, 0)
    return pl.pallas_call(
        backward_kernel,
        grid=(2 * steps,),
        out_shape=(
            jax.ShapeDtypeStruct((width, tokens), jnp.bfloat16),
            jax.ShapeDtypeStruct((nb, wide, bo), jnp.bfloat16),
            jax.ShapeDtypeStruct((nb, bi, bo), jnp.bfloat16),
        ),
        in_specs=[
            whole((width, tokens)),
            whole((width, tokens)),
            pl.BlockSpec((None, group, wide, bo), slot_second),
            pl.BlockSpec((None, group, bi, bo), slot_first),
            whole((width, tokens)),
            pl.BlockSpec((group * bo, tokens), first2),
            pl.BlockSpec((group * bo, tokens), first2),
        ],
        out_specs=(
            whole((width, tokens)),
            pl.BlockSpec((group, wide, bo), second),
            pl.BlockSpec((group, bi, bo), first),
        ),
        scratch_shapes=[
            pltpu.VMEM((nb * bo, tokens), jnp.float32),
            pltpu.VMEM((width, tokens), jnp.float32),
            pltpu.VMEM((8, tokens), jnp.float32),
            pltpu.VMEM((8, tokens), jnp.float32),
        ],
        compiler_params=pltpu.CompilerParams(vmem_limit_bytes=VMEM_BYTES),
        name="layer_backward",
    )(x, g, w_in, w_out, gain, act, slope)


def spare_buffers(shape, count):
    return pl.pallas_call(
        lambda *refs: None,
        out_shape=(jax.ShapeDtypeStruct(shape, jnp.bfloat16),) * count,
        out_specs=(pl.BlockSpec(memory_space=pl.ANY),) * count,
        name="spare_buffers",
    )()


def to_columns(a):
    micro, rows, width = a.shape
    return a.reshape(micro * rows, width).T


def per_device(inputs, cotangent, w_in, w_out, gains, counts):
    segment_count = lax.axis_size("segment")
    my_segment = lax.axis_index("segment")
    slot_count = w_in.shape[1]
    micro, rows, width = inputs.shape
    tokens = micro * rows
    count_here = jnp.sum(jnp.where(jnp.arange(segment_count) == my_segment, counts, 0))
    dp = lax.axis_size("dp")
    own_nb, bi, bo = w_in.shape[2:]
    nb = own_nb * dp
    extra = 16
    gain_rows = jnp.pad(
        gains.reshape(slot_count, own_nb, 1, bi), ((0, 0), (0, 0), (0, extra - 1), (0, bo - bi))
    )
    full_out, full_in = gather_weights(
        w_out[0], jnp.concatenate([w_in[0], gain_rows], axis=2), dp
    )
    gain = [
        jnp.broadcast_to(full_in[l, :, bi, :bi].reshape(width, 1), (width, tokens))
        for l in range(slot_count)
    ]
    first_x = to_columns(inputs)
    last_g = to_columns(cotangent)

    def run_forward(operands):
        x, saved = operands
        kept = []
        for l in range(slot_count):
            def live(x, l=l):
                return forward_layer(l, x, full_in, full_out, gain[l])

            if l == 0:
                y, act, slope = live(x)
            else:
                y, act, slope = lax.cond(
                    l < count_here, live, lambda x, l=l: (x, saved[l][1], saved[l][2]), x
                )
            kept.append((x, act, slope))
            x = y
        return x, tuple(kept)

    def keep(operands):
        return operands

    spare = spare_buffers((nb * bo, tokens), 2 * slot_count)
    saved = tuple(
        (first_x, spare[2 * l], spare[2 * l + 1]) for l in range(slot_count)
    )
    x = first_x
    result = x
    for k in range(segment_count):
        x, saved = lax.cond(my_segment == k, run_forward, keep, (x, saved))
        result = jnp.where(my_segment == k, x, result)
        if k < segment_count - 1:
            x = lax.ppermute(x, "segment", [(k, k + 1)])

    def run_backward(operands):
        g, grads = operands
        out = [None] * slot_count
        for l in reversed(range(slot_count)):
            x, act, slope = saved[l]

            def live(g, l=l, x=x, act=act, slope=slope):
                return backward_layer(l, x, g, full_in, full_out, gain[l], act, slope)

            if l == 0:
                g, *out[l] = live(g)
            else:
                g, *out[l] = lax.cond(l < count_here, live, lambda g, l=l: (g, *grads[l]), g)
        return g, tuple(tuple(o) for o in out)

    zero_in = jnp.zeros((nb, bi + extra, bo), jnp.bfloat16)
    zero_out = jnp.zeros((nb, bi, bo), jnp.bfloat16)
    grads = tuple((zero_in, zero_out) for l in range(slot_count))
    g = last_g
    down = g
    for k in reversed(range(segment_count)):
        g, grads = lax.cond(my_segment == k, run_backward, keep, (g, grads))
        down = jnp.where(my_segment == k, g, down)
        if k > 0:
            g = lax.ppermute(g, "segment", [(k, k - 1)])

    sum_out, sum_in = scatter_grads(
        [grads[l][1] for l in range(slot_count)],
        [grads[l][0] for l in range(slot_count)],
        dp,
    )
    grad_in = sum_in[None, :, :, :bi, :]
    grad_out = sum_out[None]
    grad_gain = sum_in[:, :, bi, :bi].reshape(1, slot_count, own_nb * bi)
    outputs = result.T.reshape(1, micro, rows, width)
    grads_kept = down.T.reshape(1, micro, rows, width)
    return outputs, grads_kept, grad_in, grad_out, grad_gain


def solution(mesh):
    in_specs = (
        P(None, "dp", None),
        P(None, "dp", None),
        P("segment", None, "dp", None, None),
        P("segment", None, "dp", None, None),
        P("segment", None, "dp"),
        P(),
    )
    out_specs = (
        P("segment", None, "dp", None),
        P("segment", None, "dp", None),
        P("segment", None, "dp", None, None),
        P("segment", None, "dp", None, None),
        P("segment", None, "dp"),
    )
    return jax.shard_map(
        per_device, mesh=mesh, in_specs=in_specs, out_specs=out_specs, check_vma=False
    )
```
